32 devices in a mesh: dp: 4 (over y, core), seq: 8 (over z, x).
Axes of the slice: x: 2, y: 2, z: 4, core: 2. Of those that a mesh axis runs over, the one named last changes fastest.
Arguments:
- tokens: bfloat16 [4, 2048, 2048], P('dp', 'seq'), may hold values from -6 to 6
- cotangent: bfloat16 [4, 2048, 2048], P('dp', 'seq'), may hold values from -6 to 6
- lengths: int32 [4, 4], replicated, may hold values from 256 to 1024, as said below
- placement: int32 [4], replicated, may hold values from 0 to 3, each once
- w_query: bfloat16 [2048, 2048], P(('dp', 'seq')), may hold values from -0.125 to 0.125
- w_key: bfloat16 [2048, 2048], P(('dp', 'seq')), may hold values from -0.125 to 0.125
- w_value: bfloat16 [2048, 2048], P(('dp', 'seq')), may hold values from -0.125 to 0.125
- w_output: bfloat16 [2048, 2048], P(('dp', 'seq')), may hold values from -0.125 to 0.125
- query_gain: bfloat16 [2048], P(('dp', 'seq')), may hold values from 0.099609375 to 1.8984375
- key_gain: bfloat16 [2048], P(('dp', 'seq')), may hold values from 0.099609375 to 1.8984375
- attn_gain: bfloat16 [2048], P(('dp', 'seq')), may hold values from 0.099609375 to 1.8984375
- w_gate: bfloat16 [2048, 8192], P('dp', 'seq'), may hold values from -0.125 to 0.125
- w_up: bfloat16 [2048, 8192], P('dp', 'seq'), may hold values from -0.125 to 0.125
- w_down: bfloat16 [8192, 2048], P('seq', 'dp'), may hold values from -0.0625 to 0.0625
- mlp_gain: bfloat16 [2048], P(('dp', 'seq')), may hold values from 0.099609375 to 1.8984375
Outputs:
- layer_out: bfloat16 [4, 2048, 2048], P('dp', 'seq')
- grad_tokens: bfloat16 [4, 2048, 2048], P('dp', 'seq')
- grad_query: float32 [2048, 2048], P(('dp', 'seq'))
- grad_key: float32 [2048, 2048], P(('dp', 'seq'))
- grad_value: float32 [2048, 2048], P(('dp', 'seq'))
- grad_output: float32 [2048, 2048], P(('dp', 'seq'))
- grad_query_gain: float32 [2048], P(('dp', 'seq'))
- grad_key_gain: float32 [2048], P(('dp', 'seq'))
- grad_attn_gain: float32 [2048], P(('dp', 'seq'))
- grad_gate: float32 [2048, 8192], P('dp', 'seq')
- grad_up: float32 [2048, 8192], P('dp', 'seq')
- grad_down: float32 [8192, 2048], P('seq', 'dp')
- grad_mlp_gain: float32 [2048], P(('dp', 'seq'))
The draws below stay inside these ranges and needn't reach their ends.
Inputs may be any that keep to these rules, and one draw needn't show every extreme that they name: In every row the 4 lengths sum to 2048; one of them is 1024 and another 2048 // 8. `placement`: each stored row is held at exactly one data position.
All inputs are finite; a program needn't handle non-finite values.
Results may differ from the reference program's by a relative error of at most 0.019.
Values may be sent and summed in bfloat16 or wider, within the bound.
No kernel may reach another device: no remote copies, remote signals or barrier semaphores. Data moves between devices by JAX's collectives and lax.ppermute only.
A program may use at most 320 MiB of HBM per device.

```python
import jax
import jax.numpy as jnp
from jax import lax

D = 2048
HEADS = 16
HEAD = 128
FF = 8192
ROW = 2048
DOCS = 4
ROWS = 4


def draw_lengths(key, part):
    key = jax.random.fold_in(key, 7)
    split_key, order_key = jax.random.split(key)
    eighth = ROW // 8
    extra = jax.random.randint(split_key, (ROWS,), 0, eighth + 1, dtype=jnp.int32)
    fixed_half = jnp.full((ROWS,), ROW // 2, dtype=jnp.int32)
    fixed_eighth = jnp.full((ROWS,), eighth, dtype=jnp.int32)
    pieces = jnp.stack([fixed_half, fixed_eighth, eighth + extra, 2 * eighth - extra], axis=1)
    order = jax.vmap(lambda row_key: jax.random.permutation(row_key, DOCS))(jax.random.split(order_key, ROWS))
    return jnp.take_along_axis(pieces, order.astype(jnp.int32), axis=1).astype(jnp.int32)


def strengthened(result, own_key, source, target, shards_of, factor):
    def block_of(dim):
        return (jnp.arange(result.shape[dim]) // (result.shape[dim] // shards_of)).reshape((-1,) + (1,) * (result.ndim - 1 - dim))

    first = jax.random.permutation(own_key, shards_of)[block_of(target)]
    second = (block_of(target) + shards_of // 2) % shards_of
    return jnp.where((block_of(source) == first) | (block_of(source) == second), factor * result, result)


def steps_of(rng, extent, shards, low, top_value):
    loudness, own = 1.0, jax.random.fold_in(rng, 6)
    for dim, shards_of in shards:
        draws = jnp.exp(jax.random.uniform(jax.random.fold_in(own, dim), (shards_of,), jnp.float32, low / len(shards), top_value / len(shards)))
        loudness = loudness * jnp.repeat(draws, extent[dim] // shards_of).reshape([-1 if axis == dim else 1 for axis in range(len(extent))])
    return loudness


def scatter_about(stream_key, dims, scale, bound, cuts=(), held_as=jnp.bfloat16):
    factor_of = steps_of(stream_key, dims, cuts, -0.22, 0.18) if cuts else 1.0
    result = jax.random.normal(stream_key, dims, jnp.float32) * scale * factor_of
    return jnp.minimum(jnp.maximum(result, -bound), bound).astype(held_as)


def heavy_noise(own_key, shape, width, limit, cuts, heavy, kind=jnp.bfloat16):
    array = width * jax.random.normal(own_key, shape, jnp.float32)
    if cuts:
        array = array * steps_of(own_key, shape, cuts, -0.22, 0.18)
    return jnp.clip(strengthened(array, jax.random.fold_in(own_key, 3), *heavy), -limit, limit).astype(kind)


def setup_inputs(seed: int = 0) -> dict:
    streams_of = jax.random.split(jax.random.key(seed), 16)
    return {
        "tokens": heavy_noise(streams_of[0], (ROWS, ROW, D), 1.0, 6.0, ((0, 4), (1, 8)), (1, 2, 8, 2.0)),
        "cotangent": scatter_about(streams_of[1], (ROWS, ROW, D), 1.0, 6.0, ((0, 4), (1, 8))),
        "lengths": draw_lengths(jax.random.fold_in(streams_of[15], 71), 0),
        "placement": jax.random.permutation(streams_of[3], ROWS).astype(jnp.int32),
        "w_query": scatter_about(streams_of[4], (D, D), D ** -0.5, 0.125, ((0, 32),)),
        "w_key": scatter_about(streams_of[5], (D, D), D ** -0.5, 0.125, ((0, 32),)),
        "w_value": scatter_about(streams_of[6], (D, D), D ** -0.5, 0.125, ((0, 32),)),
        "w_output": scatter_about(streams_of[7], (D, D), D ** -0.5, 0.125, ((0, 32),)),
        "query_gain": jnp.clip(1.0 + 0.18 * jax.random.normal(streams_of[8], (D,), jnp.float32), 0.099609375, 1.8984375).astype(jnp.bfloat16),
        "key_gain": jnp.clip(1.0 + 0.18 * jax.random.normal(streams_of[9], (D,), jnp.float32), 0.099609375, 1.8984375).astype(jnp.bfloat16),
        "attn_gain": jnp.clip(1.0 + 0.18 * jax.random.normal(streams_of[10], (D,), jnp.float32), 0.099609375, 1.8984375).astype(jnp.bfloat16),
        "w_gate": scatter_about(streams_of[11], (D, FF), D ** -0.5, 0.125, ((0, 4), (1, 8))),
        "w_up": scatter_about(streams_of[12], (D, FF), D ** -0.5, 0.125, ((0, 4), (1, 8))),
        "w_down": scatter_about(streams_of[13], (FF, D), FF ** -0.5, 0.0625, ((0, 8), (1, 4))),
        "mlp_gain": jnp.clip(1.0 + 0.18 * jax.random.normal(streams_of[14], (D,), jnp.float32), 0.099609375, 1.8984375).astype(jnp.bfloat16),
    }


EPSILON = 1e-06
ROPE_BASE = 500000.0
HIGHEST = lax.Precision.HIGHEST

@jax.custom_vjp
def low(v):
    return lax.optimization_barrier(v.astype(jnp.bfloat16)).astype(jnp.float32)

@jax.custom_vjp
def low_back(v):
    return v

def low_keep(v):
    return (low(v), None)

def low_pass(kept, grad):
    return (grad,)

def back_keep(v):
    return (v, None)

def back_low(kept, grad):
    return (low(grad),)
low.defvjp(low_keep, low_pass)
low_back.defvjp(back_keep, back_low)

def product(left, right):
    return jnp.dot(left, right, precision=HIGHEST)

def rms_scale(vals):
    return lax.rsqrt(lax.optimization_barrier(jnp.mean(vals * vals, axis=-1, keepdims=True)) + EPSILON)

def row_layout(doc_lens):
    positions = jnp.arange(ROW, dtype=jnp.int32)
    doc_ends = jnp.cumsum(doc_lens)
    doc_ids = lax.optimization_barrier(jnp.sum((positions[:, None] >= doc_ends[None, :]).astype(jnp.int32), axis=1))
    doc_starts = doc_ends - doc_lens
    picks = doc_ids[:, None] == jnp.arange(DOCS, dtype=jnp.int32)[None, :]
    doc_first = lax.optimization_barrier(jnp.sum(jnp.where(picks, doc_starts[None, :], 0), axis=1))
    return (doc_ids, positions - doc_first)

def rotate(vals, positions):
    half = HEAD // 2
    freq = ROPE_BASE ** (-2.0 * jnp.arange(half, dtype=jnp.float32) / HEAD)
    angle = positions.astype(jnp.float32)[:, None] * freq[None, :]
    cosine = jnp.cos(angle)[:, None, :]
    sine = jnp.sin(angle)[:, None, :]
    first = vals[..., :half]
    second = vals[..., half:]
    return jnp.concatenate([first * cosine - second * sine, second * cosine + first * sine], axis=-1)

def attend(query_rot, key_rot, values, doc_ids):
    block = min(512, ROW)
    scale = HEAD ** (-0.5)
    keys_at = jnp.arange(ROW, dtype=jnp.int32)

    def one_block(index):
        start = index * block
        query_blk = lax.dynamic_slice_in_dim(query_rot, start, block, 0)
        doc_blk = lax.dynamic_slice_in_dim(doc_ids, start, block, 0)
        rows_at = start + jnp.arange(block, dtype=jnp.int32)
        scores = jnp.einsum('qhd,khd->hqk', query_blk, key_rot, precision=HIGHEST) * scale
        scores = low_back(scores)
        allowed = (doc_blk[:, None] == doc_ids[None, :]) & (keys_at[None, :] <= rows_at[:, None])
        scores = jnp.where(allowed[None], scores, -1e+30)
        top = lax.optimization_barrier(jnp.max(scores, axis=-1, keepdims=True))
        expo = jnp.exp(scores - top)
        probs = expo / lax.optimization_barrier(jnp.sum(expo, axis=-1, keepdims=True))
        return jnp.einsum('hqk,khd->qhd', low(probs), values, precision=HIGHEST)
    outputs = lax.map(jax.checkpoint(one_block), jnp.arange(ROW // block, dtype=jnp.int32))
    return outputs.reshape(ROW, HEADS, HEAD)

def layer_row(params, inputs, doc_ids, positions):
    w_query, w_key, w_value, w_output, query_gain, key_gain, attn_gain, w_gate, w_up, w_down, mlp_gain = params
    query_pre = low_back(product(inputs, w_query))
    key_pre = low_back(product(inputs, w_key))
    values = low_back(low(product(inputs, w_value)))
    query_norm = query_pre * rms_scale(query_pre) * query_gain
    key_norm = key_pre * rms_scale(key_pre) * key_gain
    query_rot = low_back(low(rotate(query_norm.reshape(ROW, HEADS, HEAD), positions)))
    key_rot = low_back(low(rotate(key_norm.reshape(ROW, HEADS, HEAD), positions)))
    attn_heads = attend(query_rot, key_rot, values.reshape(ROW, HEADS, HEAD), doc_ids)
    attn_tokens = low_back(low(attn_heads.reshape(ROW, D)))
    attn_pre = low_back(product(attn_tokens, w_output))
    middle = inputs + attn_pre * rms_scale(attn_pre) * attn_gain
    middle_low = low(middle)
    gate_pre = low_back(product(middle_low, w_gate))
    up_pre = low_back(product(middle_low, w_up))
    hidden = low(gate_pre * jax.nn.sigmoid(gate_pre) * up_pre)
    mlp_pre = low_back(product(hidden, w_down))
    return middle + mlp_pre * rms_scale(mlp_pre) * mlp_gain

def reference(tokens, cotangent, lengths, placement, w_query, w_key, w_value, w_output, query_gain, key_gain, attn_gain, w_gate, w_up, w_down, mlp_gain):
    params = tuple((w.astype(jnp.float32) for w in (w_query, w_key, w_value, w_output, query_gain, key_gain, attn_gain, w_gate, w_up, w_down, mlp_gain)))
    zeros = tuple((jnp.zeros_like(w) for w in params))

    def step(totals, index):
        inputs = tokens[index].astype(jnp.float32)
        doc_lens = lengths[placement[index]]
        doc_ids, positions = row_layout(doc_lens)
        out_row, pull = jax.vjp(lambda chosen, given: layer_row(chosen, given, doc_ids, positions), params, inputs)
        grad_params, grad_row = pull(cotangent[index].astype(jnp.float32))
        totals = jax.tree.map(lambda left, right: left + right, totals, grad_params)
        return (totals, (out_row.astype(jnp.bfloat16), grad_row.astype(jnp.bfloat16)))
    totals, (layer_out, grad_tokens) = lax.scan(step, zeros, jnp.arange(ROWS, dtype=jnp.int32))
    grad_query, grad_key, grad_value, grad_output, grad_query_gain, grad_key_gain, grad_attn_gain, grad_gate, grad_up, grad_down, grad_mlp_gain = totals
    return (layer_out, grad_tokens, grad_query, grad_key, grad_value, grad_output, grad_query_gain, grad_key_gain, grad_attn_gain, grad_gate, grad_up, grad_down, grad_mlp_gain)
```

```python
import jax
import jax.numpy as jnp
from jax import lax
from jax.sharding import PartitionSpec as P

HEAD = 128
RING = 4
LEVELS = 4
EPSILON = 1e-06
ROPE_BASE = 500000.0
LOW = jnp.bfloat16
FULL = jnp.float32


def dot(left, right):
    return jnp.dot(left, right, preferred_element_type=FULL)


def dot_nt(left, right):
    return lax.dot_general(left, right, (((1,), (1,)), ((), ())), preferred_element_type=FULL)


def dot_tn(left, right):
    return lax.dot_general(left, right, (((0,), (0,)), ((), ())), preferred_element_type=FULL)


def swap(val, axis, mask):
    size = lax.axis_size(axis)
    return lax.ppermute(val, axis, [(i, i ^ mask) for i in range(size)])


def swap_all(val, mask):
    size = lax.axis_size("dp") * lax.axis_size("seq")
    return lax.ppermute(val, ("dp", "seq"), [(i, i ^ mask) for i in range(size)])


def bits_of(size):
    return [1 << i for i in range(size.bit_length() - 1)]


def sum_over(val, axis, size):
    for bit in bits_of(size):
        val = val + swap(val, axis, bit)
    return val


class Ring:
    def __init__(self, cycles):
        self.size = len(cycles[0])
        self.forth = [(c[i], c[(i + 1) % self.size]) for c in cycles for i in range(self.size)]
        self.back = [(b, a) for a, b in self.forth]
        total = self.size * len(cycles)
        owners = [[0] * self.size for _ in range(total)]
        for c in cycles:
            for i, dev in enumerate(c):
                for off in range(self.size):
                    owners[dev][off] = c[(i + off) % self.size]
        self.owners = owners

    def owner(self, offset):
        table = jnp.array([row[offset % self.size] for row in self.owners], jnp.int32)
        return lax.dynamic_index_in_dim(table, lax.axis_index("seq"), 0, False)

    def right(self, val):
        return lax.ppermute(val, "seq", self.forth)

    def left(self, val):
        return lax.ppermute(val, "seq", self.back)

    def gather(self, own):
        half = self.size // 2
        chunks = {0: own}
        r = l = own
        for k in range(1, half):
            r, l = self.right(r), self.left(l)
            chunks[-k], chunks[k] = r, l
        mid = own.shape[0] // 2
        chunks[half] = jnp.concatenate([self.right(r[:mid]), self.left(l[mid:])], axis=0)
        return chunks

    def scatter(self, part):
        half = self.size // 2
        far = part(half).astype(LOW)
        mid = far.shape[0] // 2
        r, l = self.right(far[:mid]), self.left(far[mid:])
        zero = jnp.zeros((), LOW)
        r = lax.pad(r, zero, ((0, mid, 0), (0, 0, 0)))
        l = lax.pad(l, zero, ((mid, 0, 0), (0, 0, 0)))
        for k in range(half - 1, 0, -1):
            a = part(k) + r.astype(FULL)
            b = part(-k) + l.astype(FULL)
            r, l = self.right(a.astype(LOW)), self.left(b.astype(LOW))
        return part(0) + r.astype(FULL) + l.astype(FULL)


def row_cycle(size):
    if size % LEVELS or size == LEVELS:
        return list(range(size))
    cols = size // LEVELS
    walk = [(0, 0)]
    for z in range(LEVELS):
        span = list(range(1, cols))
        walk += [(z, x) for x in (span if z % 2 == 0 else span[::-1])]
    walk += [(z, 0) for z in range(LEVELS - 1, 0, -1)]
    return [z * cols + x for z, x in walk]


def block_cycles(size):
    order = [0, 1, 3, 2] if size // LEVELS == 2 else [0, 1, 2, 3]
    return [[base + i for i in order] for base in range(0, size, RING)]


def data_bits(size):
    return [b for b in bits_of(size) if b != 1] + [1]


def copies_over_data(shard, size):
    copies = [(0, shard)]
    for bit in data_bits(size):
        copies = copies + [(mask ^ bit, swap(val, "dp", bit)) for mask, val in copies]
    return copies


def gather_over_data(shard, axis):
    size = lax.axis_size("dp")
    me = lax.axis_index("dp")
    shape = list(shard.shape)
    shape[axis] *= size
    whole = jnp.zeros(shape, shard.dtype)
    for mask, val in copies_over_data(shard, size):
        start = [0] * len(shape)
        start[axis] = (me ^ mask) * shard.shape[axis]
        whole = lax.dynamic_update_slice(whole, val, start)
    return whole


def scatter_over_data(whole):
    size = lax.axis_size("dp")
    me = lax.axis_index("dp")
    rest = whole.shape[1:]
    order = data_bits(size)[::-1]
    whole = whole.reshape((2,) * len(bits_of(size)) + rest)
    left = sorted(bits_of(size), reverse=True)
    for step, bit in enumerate(order):
        dim = left.index(bit)
        left.remove(bit)
        mine = (me // bit) % 2
        kept = lax.dynamic_index_in_dim(whole, mine, dim, False)
        sent = lax.dynamic_index_in_dim(whole, 1 - mine, dim, False)
        got = swap(sent, "dp", bit)
        whole = kept.astype(FULL) + got.astype(FULL)
        if step < len(order) - 1:
            whole = whole.astype(LOW)
    return whole


def gather_gains(gains):
    total = lax.axis_size("dp") * lax.axis_size("seq")
    me = lax.axis_index("dp") * lax.axis_size("seq") + lax.axis_index("seq")
    val = gains[None]
    for bit in bits_of(total):
        got = swap_all(val, bit)
        upper = (me // bit) % 2 == 1
        val = jnp.concatenate([jnp.where(upper, got, val), jnp.where(upper, val, got)], axis=0)
    return jnp.moveaxis(val, 0, 1).reshape(gains.shape[0], -1)


def gather_output_weights(w_output, row_ring):
    data, seq = lax.axis_size("dp"), lax.axis_size("seq")
    me = lax.axis_index("dp")
    rows, width = w_output.shape
    tall = data // 2
    stack = w_output[None]
    for bit in data_bits(data)[:-1]:
        got = swap(stack, "dp", bit)
        upper = (me // bit) % 2 == 1
        stack = jnp.concatenate([jnp.where(upper, got, stack), jnp.where(upper, stack, got)], axis=0)
    chunks = row_ring.gather(stack.reshape(tall * rows, width))
    whole = jnp.zeros((tall, 2, seq, rows, width), w_output.dtype)
    for offset, chunk in chunks.items():
        owner = row_ring.owner(offset)
        other = swap(chunk, "dp", 1)
        for core, val in ((me % 2, chunk), (1 - me % 2, other)):
            val = val.reshape(tall, 1, 1, rows, width)
            whole = lax.dynamic_update_slice(whole, val, (0, core, owner, 0, 0))
    return whole.reshape(data * seq * rows, width)


def scatter_output_grad(part, row_ring):
    data, seq = lax.axis_size("dp"), lax.axis_size("seq")
    me = lax.axis_index("dp")
    tall = data // 2
    width = part.shape[1]
    rows = part.shape[0] // (data * seq)
    part = part.astype(LOW).reshape(tall, 2, seq, rows, width)
    kept = lax.dynamic_index_in_dim(part, me % 2, 1, False)
    sent = lax.dynamic_index_in_dim(part, 1 - me % 2, 1, False)
    kept = (kept.astype(FULL) + swap(sent, "dp", 1).astype(FULL)).astype(LOW)

    def block(offset):
        one = lax.dynamic_index_in_dim(kept, row_ring.owner(offset), 1, False)
        return one.reshape(tall * rows, width).astype(FULL)

    val = row_ring.scatter(block).reshape(tall, rows, width)
    for bit in data_bits(data)[:-1][::-1]:
        upper = (me // bit) % 2
        val = val.reshape(2, val.shape[0] // 2, rows, width)
        kept = lax.dynamic_index_in_dim(val, upper, 0, False)
        sent = lax.dynamic_index_in_dim(val, 1 - upper, 0, False)
        val = kept + swap(sent, "dp", bit)
    return val.reshape(rows, width)


def rms_scale(vals):
    return lax.rsqrt(jnp.mean(vals * vals, axis=-1, keepdims=True) + EPSILON)


def norm_back(grad_out, pre, scale, gain):
    weighted = grad_out * gain
    inner = jnp.mean(weighted * pre, axis=-1, keepdims=True)
    grad_pre = scale * weighted - pre * (scale * scale * scale) * inner
    grad_gain = jnp.sum(grad_out * pre * scale, axis=0)
    return (grad_pre, grad_gain)


def rope_tables(positions, width):
    half = width // 2
    freq = ROPE_BASE ** (-2.0 * jnp.arange(half, dtype=FULL) / width)
    angle = positions.astype(FULL)[:, None] * freq[None, :]
    return (jnp.cos(angle)[:, None, :], jnp.sin(angle)[:, None, :])


def rotate(vals, cosine, sine):
    half = vals.shape[-1] // 2
    first = vals[..., :half]
    second = vals[..., half:]
    return jnp.concatenate(
        [first * cosine - second * sine, second * cosine + first * sine], axis=-1
    )


def layout(lengths, placement, row_len):
    stored, docs = lengths.shape
    row = lax.dynamic_index_in_dim(placement, lax.axis_index("dp"), 0, False)
    doc_lens = jnp.sum(
        jnp.where(jnp.arange(stored, dtype=jnp.int32)[:, None] == row, lengths, 0), axis=0
    )
    upto = jnp.arange(docs, dtype=jnp.int32)
    doc_ends = jnp.sum(jnp.where(upto[None, :] <= upto[:, None], doc_lens[None, :], 0), axis=1)
    at = jnp.arange(row_len, dtype=jnp.int32)
    passed = at[:, None] >= doc_ends[None, :]
    doc_ids = jnp.sum(passed.astype(jnp.int32), axis=1)
    doc_first = jnp.max(jnp.where(passed, doc_ends[None, :], 0), axis=1)
    return doc_ids, at - doc_first


def scores_of(queries, keys, doc_ids):
    at = jnp.arange(doc_ids.shape[0], dtype=jnp.int32)
    scores = jnp.einsum("qhd,khd->hqk", queries, keys, preferred_element_type=FULL) * HEAD**-0.5
    allowed = (doc_ids[:, None] == doc_ids[None, :]) & (at[None, :] <= at[:, None])
    return jnp.where(allowed[None], scores, -1e30)


def attend_forward(queries, keys, vals, doc_ids):
    scores = scores_of(queries, keys, doc_ids)
    top = jnp.max(scores, axis=-1, keepdims=True)
    expo = jnp.exp(scores - top)
    total = jnp.sum(expo, axis=-1, keepdims=True)
    probs = (expo / total).astype(LOW)
    out = jnp.einsum("hqk,khd->qhd", probs, vals, preferred_element_type=FULL)
    return out.astype(LOW), top + jnp.log(total)


def attend_backward(queries, keys, vals, doc_ids, sums, grads):
    probs = jnp.exp(scores_of(queries, keys, doc_ids) - sums)
    grad_probs = jnp.einsum("qhd,khd->hqk", grads, vals, preferred_element_type=FULL)
    inner = jnp.sum(probs * grad_probs, axis=-1, keepdims=True)
    grad_scores = (probs * (grad_probs - inner)).astype(LOW)
    scale = HEAD**-0.5
    grad_q = jnp.einsum("hqk,khd->qhd", grad_scores, keys, preferred_element_type=FULL) * scale
    grad_k = jnp.einsum("hqk,qhd->khd", grad_scores, queries, preferred_element_type=FULL) * scale
    grad_v = jnp.einsum("hqk,qhd->khd", probs.astype(LOW), grads, preferred_element_type=FULL)
    return grad_q.astype(LOW), grad_k.astype(LOW), grad_v.astype(LOW)


def per_device(
    tokens,
    cotangent,
    lengths,
    placement,
    w_query,
    w_key,
    w_value,
    w_output,
    query_gain,
    key_gain,
    attn_gain,
    w_gate,
    w_up,
    w_down,
    mlp_gain,
):
    data, seq = lax.axis_size("dp"), lax.axis_size("seq")
    seq_at = lax.axis_index("seq")
    _, count, width = tokens.shape
    row_len = count * seq
    own = width // seq
    heads = own // HEAD
    row_ring = Ring([row_cycle(seq)])
    ring = Ring(block_cycles(seq))
    sets = seq // RING
    inputs = tokens.reshape(count, width)
    doc_ids, positions = layout(lengths, placement, row_len)
    cosine, sine = rope_tables(positions, HEAD)

    packed = jnp.stack([w_query, w_key, w_value], axis=1).reshape(-1, 3, seq, own)
    packed = jnp.moveaxis(packed, 2, 0).reshape(seq, -1, 3 * own)
    packed = lax.all_to_all(packed, "seq", split_axis=0, concat_axis=0, tiled=True)
    w_heads = gather_over_data(packed.reshape(-1, 3 * own), 0)

    row_chunks = row_ring.gather(inputs)
    pre = jnp.zeros((row_len, 3 * own), FULL)
    row_tokens = jnp.zeros((row_len, width), LOW)
    for offset, chunk in row_chunks.items():
        start = row_ring.owner(offset) * count
        pre = lax.dynamic_update_slice(pre, dot(chunk, w_heads), (start, 0))
        row_tokens = lax.dynamic_update_slice(row_tokens, chunk, (start, 0))

    gains = gather_gains(jnp.stack([query_gain, key_gain, attn_gain, mlp_gain]))
    gains = gains.astype(FULL)
    gain_attn, gain_mlp = gains[2], gains[3]
    gains_own = lax.dynamic_slice(gains, (0, seq_at * own), (2, own))

    w_in = jnp.concatenate([w_gate, w_up], axis=1)
    gate_up, downs = [], []
    for k in range(sets):
        part_in = w_in if k == 0 else swap(w_in, "seq", RING * k)
        part_down = w_down if k == 0 else swap(w_down, "seq", RING * k)
        gate_up.append(gather_over_data(part_in, 0))
        downs.append(gather_over_data(part_down, 1))
    hid = w_gate.shape[1]
    w_out = gather_output_weights(w_output, row_ring)

    query_pre, key_pre, value_pre = pre[:, :own], pre[:, own : 2 * own], pre[:, 2 * own :]
    squares = jnp.stack([jnp.sum(query_pre * query_pre, axis=1), jnp.sum(key_pre * key_pre, axis=1)])
    scales = lax.rsqrt(sum_over(squares, "seq", seq) / width + EPSILON)
    query_scale, key_scale = scales[0][:, None], scales[1][:, None]

    def split(val):
        return val.reshape(row_len, heads, HEAD)

    query_rot = rotate(split(query_pre * query_scale * gains_own[0]), cosine, sine).astype(LOW)
    key_rot = rotate(split(key_pre * key_scale * gains_own[1]), cosine, sine).astype(LOW)
    values = split(value_pre.astype(LOW))
    attn_heads, log_sums = attend_forward(query_rot, key_rot, values, doc_ids)
    attn_tokens = lax.all_to_all(
        attn_heads.reshape(seq, count, own), "seq", split_axis=0, concat_axis=0, tiled=True
    )
    attn_tokens = jnp.moveaxis(attn_tokens, 0, 1).reshape(count, width)
    attn_pre = dot(attn_tokens, w_out)
    attn_scale = rms_scale(attn_pre)
    middle = inputs.astype(FULL) + attn_pre * attn_scale * gain_attn
    middle_low = middle.astype(LOW)

    mids = ring.gather(middle_low)
    saved = {}

    def mlp_part(offset):
        offset = offset if offset in mids else -offset
        total = 0.0
        for k in range(sets):
            both = dot(mids[offset], gate_up[k])
            gate, up = both[:, :hid], both[:, hid:]
            hidden = (gate * jax.nn.sigmoid(gate) * up).astype(LOW)
            saved[offset, k] = gate, up, hidden
            total = total + dot(hidden, downs[k])
        return total

    mlp_pre = ring.scatter(mlp_part)
    mlp_scale = rms_scale(mlp_pre)
    layer_out = (middle + mlp_pre * mlp_scale * gain_mlp).astype(LOW).reshape(tokens.shape)
    grad_final = cotangent.reshape(count, width).astype(FULL)
    grad_mlp_pre, grad_gain_mlp = norm_back(grad_final, mlp_pre, mlp_scale, gain_mlp)
    grads = ring.gather(grad_mlp_pre.astype(LOW))
    grad_both = {}

    def middle_part(offset):
        offset = offset if offset in mids else -offset
        total = 0.0
        for k in range(sets):
            gate, up, hidden = saved[offset, k]
            grad_hidden = dot_nt(grads[offset], downs[k])
            sig = jax.nn.sigmoid(gate)
            grad_gate = grad_hidden * up * sig * (1.0 + gate * (1.0 - sig))
            grad_up = grad_hidden * gate * sig
            both = jnp.concatenate([grad_gate.astype(LOW), grad_up.astype(LOW)], axis=1)
            grad_both[offset, k] = both
            total = total + dot_nt(both, gate_up[k])
        return total

    grad_middle = grad_final + ring.scatter(middle_part)
    order = list(mids)
    mid_rows = jnp.concatenate([mids[o] for o in order])
    grad_rows = jnp.concatenate([grads[o] for o in order])
    grad_in, grad_down = 0.0, 0.0
    for k in reversed(range(sets)):
        hidden = jnp.concatenate([saved[o, k][2] for o in order])
        both = jnp.concatenate([grad_both[o, k] for o in order])
        part_down = dot_tn(hidden, grad_rows).astype(LOW).reshape(hid, data, width // data)
        part_down = scatter_over_data(jnp.moveaxis(part_down, 1, 0))
        part_in = dot_tn(mid_rows, both).astype(LOW).reshape(data, width // data, 2 * hid)
        part_in = scatter_over_data(part_in)
        if k:
            part_down = swap(part_down.astype(LOW), "seq", RING * k).astype(FULL)
            part_in = swap(part_in.astype(LOW), "seq", RING * k).astype(FULL)
        grad_down = grad_down + part_down
        grad_in = grad_in + part_in
    grad_gate, grad_up = grad_in[:, :hid], grad_in[:, hid:]

    grad_attn_pre, grad_gain_attn = norm_back(grad_middle, attn_pre, attn_scale, gain_attn)
    grad_attn_low = grad_attn_pre.astype(LOW)
    grad_heads = dot_nt(grad_attn_low, w_out).astype(LOW).reshape(count, seq, own)
    grad_heads = lax.all_to_all(
        jnp.moveaxis(grad_heads, 1, 0), "seq", split_axis=0, concat_axis=0, tiled=True
    )
    grad_heads = split(grad_heads)
    grad_output = scatter_output_grad(dot_tn(attn_tokens, grad_attn_low), row_ring)
    grad_q, grad_k, grad_v = attend_backward(
        query_rot, key_rot, values, doc_ids, log_sums, grad_heads
    )
    grad_q = rotate(grad_q.astype(FULL), cosine, -sine).reshape(row_len, own)
    grad_k = rotate(grad_k.astype(FULL), cosine, -sine).reshape(row_len, own)
    weighted_q, weighted_k = grad_q * gains_own[0], grad_k * gains_own[1]
    inner = jnp.stack(
        [jnp.sum(weighted_q * query_pre, axis=1), jnp.sum(weighted_k * key_pre, axis=1)]
    )
    inner = sum_over(inner, "seq", seq) / width
    grad_qp = query_scale * weighted_q - query_pre * (query_scale**3) * inner[0][:, None]
    grad_kp = key_scale * weighted_k - key_pre * (key_scale**3) * inner[1][:, None]
    grad_pre = jnp.concatenate(
        [grad_qp.astype(LOW), grad_kp.astype(LOW), grad_v.reshape(row_len, own)], axis=1
    )

    def token_part(offset):
        start = row_ring.owner(offset) * count
        return dot_nt(lax.dynamic_slice_in_dim(grad_pre, start, count, 0), w_heads)

    grad_tokens = (grad_middle + row_ring.scatter(token_part)).astype(LOW).reshape(tokens.shape)
    part = dot_tn(row_tokens, grad_pre).astype(LOW).reshape(data, width // data, 3 * own)
    part = scatter_over_data(part).astype(LOW)
    part = lax.all_to_all(
        part.reshape(seq, -1, 3 * own), "seq", split_axis=0, concat_axis=0, tiled=True
    ).astype(FULL)
    part = jnp.moveaxis(part.reshape(seq, -1, 3, own), 0, 2).reshape(-1, 3, width)

    placed = lax.dynamic_update_slice(
        jnp.zeros((2, width), FULL),
        jnp.stack(
            [
                jnp.sum(grad_q * query_pre * query_scale, axis=0),
                jnp.sum(grad_k * key_pre * key_scale, axis=0),
            ]
        ),
        (0, seq_at * own),
    )
    placed = jnp.concatenate([placed, grad_gain_attn[None], grad_gain_mlp[None]])
    for bit in bits_of(data * seq):
        placed = placed + swap_all(placed, bit)
    share = width // (data * seq)
    start = (lax.axis_index("dp") * seq + seq_at) * share
    gain_grads = lax.dynamic_slice(placed, (0, start), (4, share))

    return (
        layer_out,
        grad_tokens,
        part[:, 0],
        part[:, 1],
        part[:, 2],
        grad_output,
        gain_grads[0],
        gain_grads[1],
        gain_grads[2],
        grad_gate,
        grad_up,
        grad_down,
        gain_grads[3],
    )


def solution(mesh):
    rows = P("dp", "seq", None)
    both = P(("dp", "seq"), None)
    flat = P(("dp", "seq"))
    return jax.shard_map(
        per_device,
        mesh=mesh,
        in_specs=(rows, rows, P(), P())
        + (both,) * 4
        + (flat,) * 3
        + (P("dp", "seq"), P("dp", "seq"), P("seq", "dp"), flat),
        out_specs=(rows, rows)
        + (both,) * 4
        + (flat,) * 3
        + (P("dp", "seq"), P("dp", "seq"), P("seq", "dp"), flat),
        check_vma=False,
    )
```

```python
import math

import jax
import jax.numpy as jnp
from jax import lax
from jax.experimental import pallas as pl
from jax.experimental.pallas import tpu as pltpu
from jax.sharding import PartitionSpec as P

HEAD = 128
LEVELS = 4
EPSILON = 1e-06
ROPE_BASE = 500000.0
LOW = jnp.bfloat16
FULL = jnp.float32
NEG = -1e30
LOG2E = math.log2(math.e)
BLOCK = 512


def dot(left, right):
    return jnp.dot(left, right, preferred_element_type=FULL)


def dot_nt(left, right):
    return lax.dot_general(left, right, (((1,), (1,)), ((), ())), preferred_element_type=FULL)


def dot_tn(left, right):
    return lax.dot_general(left, right, (((0,), (0,)), ((), ())), preferred_element_type=FULL)


def swap(val, axis, mask):
    size = lax.axis_size(axis)
    return lax.ppermute(val, axis, [(i, i ^ mask) for i in range(size)])


def swap_all(val, mask):
    size = lax.axis_size("dp") * lax.axis_size("seq")
    return lax.ppermute(val, ("dp", "seq"), [(i, i ^ mask) for i in range(size)])


def after(vals, *first):
    return lax.optimization_barrier((vals, first))[0]


def bits_of(size):
    return [1 << i for i in range(size.bit_length() - 1)]


def sum_over(val, axis, size):
    for bit in bits_of(size):
        val = val + swap(val, axis, bit)
    return val


class Ring:
    def __init__(self, cycles):
        self.size = len(cycles[0])
        self.forth = [(c[i], c[(i + 1) % self.size]) for c in cycles for i in range(self.size)]
        self.back = [(b, a) for a, b in self.forth]
        total = self.size * len(cycles)
        owners = [[0] * self.size for _ in range(total)]
        for c in cycles:
            for i, dev in enumerate(c):
                for off in range(self.size):
                    owners[dev][off] = c[(i + off) % self.size]
        self.owners = owners

    def owner(self, offset):
        table = jnp.array([row[offset % self.size] for row in self.owners], jnp.int32)
        return lax.dynamic_index_in_dim(table, lax.axis_index("seq"), 0, False)

    def right(self, val):
        return lax.ppermute(val, "seq", self.forth)

    def left(self, val):
        return lax.ppermute(val, "seq", self.back)

    def gather(self, own, between=None):
        half = self.size // 2
        chunks = {0: own}
        r = l = own
        for k in range(1, half):
            beside = between(k) if between else ()
            r, l = self.right(r), self.left(l)
            chunks[-k], chunks[k] = r, l
            r, l = after((r, l), beside)
        mid = own.shape[0] // 2
        chunks[half] = jnp.concatenate([self.right(r[:mid]), self.left(l[mid:])], axis=0)
        return chunks

    def scatter(self, part):
        half = self.size // 2
        far = part(half).astype(LOW)
        mid = far.shape[0] // 2
        r, l = self.right(far[:mid]), self.left(far[mid:])
        zero = jnp.zeros((), LOW)
        r = lax.pad(r, zero, ((0, mid, 0), (0, 0, 0)))
        l = lax.pad(l, zero, ((mid, 0, 0), (0, 0, 0)))
        for k in range(half - 1, 0, -1):
            a = part(k) + r.astype(FULL)
            b = part(-k) + l.astype(FULL)
            r, l = self.right(a.astype(LOW)), self.left(b.astype(LOW))
        return part(0) + r.astype(FULL) + l.astype(FULL)


def row_cycle(size):
    if size % LEVELS or size == LEVELS:
        return list(range(size))
    cols = size // LEVELS
    walk = [(0, 0)]
    for z in range(LEVELS):
        span = list(range(1, cols))
        walk += [(z, x) for x in (span if z % 2 == 0 else span[::-1])]
    walk += [(z, 0) for z in range(LEVELS - 1, 0, -1)]
    return [z * cols + x for z, x in walk]


def data_bits(size):
    return [b for b in bits_of(size) if b != 1] + [1]


def swap_chips(shard, bits):
    copies = {0: shard}
    for bit in bits:
        copies |= {mask ^ bit: swap(val, "dp", bit) for mask, val in copies.items()}
    return copies


def swap_cores(copies):
    return copies | {mask ^ 1: swap(val, "dp", 1) for mask, val in copies.items()}


def swap_blocks(val):
    size = lax.axis_size("dp")
    me = lax.axis_index("dp")
    part = val.shape[1] // size
    blocks = [lax.dynamic_slice_in_dim(val, (me ^ m) * part, part, 1) for m in range(size)]
    return jnp.concatenate(blocks, axis=1)


def place_over_data(copies):
    me = lax.axis_index("dp")
    rows, cols = copies[0].shape
    whole = jnp.zeros((rows * len(copies), cols), copies[0].dtype)
    for mask, val in copies.items():
        whole = lax.dynamic_update_slice(whole, val, ((me ^ mask) * rows, 0))
    return whole


def pack(gates, ups):
    rows, cols = gates[0].shape
    whole = jnp.zeros((rows * len(gates), 2 * cols), LOW)
    for mask in gates:
        whole = lax.dynamic_update_slice(whole, gates[mask], (mask * rows, 0))
        whole = lax.dynamic_update_slice(whole, ups[mask], (mask * rows, cols))
    return whole


def scatter_over_data(blocks):
    order = data_bits(len(blocks))[::-1]
    blocks = dict(enumerate(blocks))
    for step, bit in enumerate(order):
        out = {}
        for m in [m for m in blocks if not m & bit]:
            total = blocks[m].astype(FULL) + swap(blocks[m ^ bit], "dp", bit).astype(FULL)
            out[m] = total if step == len(order) - 1 else total.astype(LOW)
        blocks = out
    return blocks[0]


def gain_step(val, bit):
    me = lax.axis_index("dp") * lax.axis_size("seq") + lax.axis_index("seq")
    got = swap_all(val, bit)
    upper = (me // bit) % 2 == 1
    return jnp.concatenate([jnp.where(upper, got, val), jnp.where(upper, val, got)], axis=0)


def stack_output_weights(w_output):
    me = lax.axis_index("dp")
    stack = w_output[None]
    for bit in data_bits(lax.axis_size("dp"))[:-1]:
        got = swap(stack, "dp", bit)
        upper = (me // bit) % 2 == 1
        stack = jnp.concatenate([jnp.where(upper, got, stack), jnp.where(upper, stack, got)], axis=0)
    return stack


def gather_output_weights(stack, row_ring):
    data, seq = lax.axis_size("dp"), lax.axis_size("seq")
    me = lax.axis_index("dp")
    tall, rows, width = stack.shape
    chunks = row_ring.gather(stack.reshape(tall * rows, width))
    whole = jnp.zeros((tall, 2, seq, rows, width), stack.dtype)
    for offset, chunk in chunks.items():
        owner = row_ring.owner(offset)
        other = swap(chunk, "dp", 1)
        for core, val in ((me % 2, chunk), (1 - me % 2, other)):
            val = val.reshape(tall, 1, 1, rows, width)
            whole = lax.dynamic_update_slice(whole, val, (0, core, owner, 0, 0))
    return whole.reshape(data * seq * rows, width)


def scatter_output_grad(part, row_ring):
    data, seq = lax.axis_size("dp"), lax.axis_size("seq")
    me = lax.axis_index("dp")
    tall = data // 2
    width = part.shape[1]
    rows = part.shape[0] // (data * seq)
    part = part.astype(LOW).reshape(tall, 2, seq, rows, width)
    kept = lax.dynamic_index_in_dim(part, me % 2, 1, False)
    sent = lax.dynamic_index_in_dim(part, 1 - me % 2, 1, False)
    kept = (kept.astype(FULL) + swap(sent, "dp", 1).astype(FULL)).astype(LOW)

    def block(offset):
        one = lax.dynamic_index_in_dim(kept, row_ring.owner(offset), 1, False)
        return one.reshape(tall * rows, width).astype(FULL)

    val = row_ring.scatter(block).reshape(tall, rows, width)
    for bit in data_bits(data)[:-1][::-1]:
        upper = (me // bit) % 2
        val = val.reshape(2, val.shape[0] // 2, rows, width)
        kept = lax.dynamic_index_in_dim(val, upper, 0, False)
        sent = lax.dynamic_index_in_dim(val, 1 - upper, 0, False)
        val = kept + swap(sent, "dp", bit)
    return val.reshape(rows, width)


def rms_scale(vals):
    return lax.rsqrt(jnp.mean(vals * vals, axis=-1, keepdims=True) + EPSILON)


def norm_back(grad_out, pre, scale, gain):
    weighted = grad_out * gain
    inner = jnp.mean(weighted * pre, axis=-1, keepdims=True)
    grad_pre = scale * weighted - pre * (scale * scale * scale) * inner
    grad_gain = jnp.sum(grad_out * pre * scale, axis=0)
    return (grad_pre, grad_gain)


def rope_tables(positions):
    half = HEAD // 2
    freq = ROPE_BASE ** (-2.0 * jnp.arange(half, dtype=FULL) / HEAD)
    angle = positions.astype(FULL)[:, None] * freq[None, :]
    cosine, sine = jnp.cos(angle), jnp.sin(angle)
    return jnp.concatenate([cosine, cosine], 1), jnp.concatenate([-sine, sine], 1)


def layout(lengths, placement, row_len):
    stored, docs = lengths.shape
    row = lax.dynamic_index_in_dim(placement, lax.axis_index("dp"), 0, False)
    doc_lens = jnp.sum(
        jnp.where(jnp.arange(stored, dtype=jnp.int32)[:, None] == row, lengths, 0), axis=0
    )
    upto = jnp.arange(docs, dtype=jnp.int32)
    doc_ends = jnp.sum(jnp.where(upto[None, :] <= upto[:, None], doc_lens[None, :], 0), axis=1)
    at = jnp.arange(row_len, dtype=jnp.int32)
    passed = at[:, None] >= doc_ends[None, :]
    return jnp.max(jnp.where(passed, doc_ends[None, :], 0), axis=1)


def column(row):
    return jnp.broadcast_to(row, (HEAD, row.shape[1])).T

def attend_forward_kernel(first_ref, q_ref, k_ref, v_ref, scale_ref, gain_ref, cos_ref, sin_ref, begin_ref,
                          out_ref, qr_ref, kr_ref, vl_ref, lse_ref, vt_ref):
    blocks = q_ref.shape[0] // BLOCK
    factor = HEAD ** -0.5 * LOG2E

    def prepare(i, _):
        rows = pl.ds(pl.multiple_of(i * BLOCK, BLOCK), BLOCK)
        for n, (src, dst) in enumerate(((q_ref, qr_ref), (k_ref, kr_ref))):
            x = src[rows, :] * column(scale_ref[n : n + 1, rows]) * gain_ref[n : n + 1, :]
            x = x * cos_ref[rows, :] + pltpu.roll(x, HEAD // 2, 1) * sin_ref[rows, :]
            dst[rows, :] = x.astype(LOW)
        v = v_ref[rows, :].astype(LOW)
        vl_ref[rows, :] = v
        vt_ref[:, rows] = v.T
        return 0

    lax.fori_loop(0, blocks, prepare, 0)

    def one(i, _):
        rows = pl.ds(pl.multiple_of(i * BLOCK, BLOCK), BLOCK)
        q = qr_ref[rows, :]
        begin = begin_ref[0:1, rows]
        at = lax.broadcasted_iota(jnp.int32, (BLOCK, BLOCK), 0)
        query_at = lax.broadcasted_iota(jnp.int32, (1, BLOCK), 1) + i * BLOCK

        def step(j, carry):
            top, total, acc = carry
            keys = pl.ds(pl.multiple_of(j * BLOCK, BLOCK), BLOCK)
            s = dot_nt(kr_ref[keys, :], q)
            key_at = at + j * BLOCK
            s = jnp.where((key_at >= begin) & (key_at <= query_at), s, NEG)
            new = jnp.maximum(top, jnp.max(s, axis=0, keepdims=True))
            p = jnp.exp2((s - new) * factor)
            shrink = jnp.exp2((top - new) * factor)
            total = total * shrink + jnp.sum(p, axis=0, keepdims=True)
            acc = acc * shrink + dot(vt_ref[:, keys], p.astype(LOW))
            return new, total, acc

        start = (jnp.full((1, BLOCK), NEG, FULL), jnp.zeros((1, BLOCK), FULL), jnp.zeros((HEAD, BLOCK), FULL))
        top, total, acc = lax.fori_loop(first_ref[i], i + 1, step, start)
        out_ref[rows, :] = (acc / total).T.astype(LOW)
        lse_ref[0, 0:1, rows] = top * factor + jnp.log2(total)
        return 0

    lax.fori_loop(0, blocks, one, 0)


def attend_forward(pre, scales, gains, cosine, sine, first, begin):
    rows, wide = pre.shape
    heads = wide // (3 * HEAD)
    col = lambda shift: pl.BlockSpec((rows, HEAD), lambda h, f: (0, h + shift))
    fixed = lambda shape: pl.BlockSpec(shape, lambda h, f: (0,) * len(shape))
    low = jax.ShapeDtypeStruct((rows, heads * HEAD), LOW)
    return pl.pallas_call(
        attend_forward_kernel,
        grid_spec=pltpu.PrefetchScalarGridSpec(
            num_scalar_prefetch=1,
            grid=(heads,),
            in_specs=[col(0), col(heads), col(2 * heads), fixed((2, rows)),
                      pl.BlockSpec((2, HEAD), lambda h, f: (0, h)), fixed((rows, HEAD)), fixed((rows, HEAD)), fixed((1, rows))],
            out_specs=[col(0)] * 4 + [pl.BlockSpec((1, 1, rows), lambda h, f: (h, 0, 0))],
            scratch_shapes=[pltpu.VMEM((HEAD, rows), LOW)],
        ),
        out_shape=[low] * 4 + [jax.ShapeDtypeStruct((heads, 1, rows), FULL)],
        compiler_params=pltpu.CompilerParams(vmem_limit_bytes=48 * 2**20),
        cost_estimate=pl.CostEstimate(flops=heads * rows * rows * HEAD * 2, bytes_accessed=rows * wide * 8, transcendentals=heads * rows * rows // 2),
        name="attend_forward",
    )(first, pre, pre, pre, scales, gains, cosine, sine, begin)


def attend_backward_kernel(first_ref, q_ref, k_ref, v_ref, o_ref, do_ref, lse_ref, qp_ref, kp_ref, scale_ref, gain_ref, cos_ref, sin_ref, begin_ref,
                           gq_ref, gk_ref, gv_ref, inner_ref, gain_grad_ref, kt_ref, dk_ref, dv_ref):
    blocks = q_ref.shape[0] // BLOCK
    norm = HEAD ** -0.5
    factor = norm * LOG2E

    def prepare(i, _):
        rows = pl.ds(pl.multiple_of(i * BLOCK, BLOCK), BLOCK)
        kt_ref[:, rows] = k_ref[rows, :].T
        dk_ref[rows, :] = jnp.zeros((BLOCK, HEAD), FULL)
        dv_ref[rows, :] = jnp.zeros((BLOCK, HEAD), FULL)
        return 0

    lax.fori_loop(0, blocks, prepare, 0)

    def finish(rows, n, grad, pre_ref, out):
        grad = grad.astype(LOW).astype(FULL)
        grad = grad * cos_ref[rows, :] - pltpu.roll(grad, HEAD // 2, 1) * sin_ref[rows, :]
        weighted = grad * gain_ref[n : n + 1, :]
        pre = pre_ref[rows, :]
        out[rows, :] = weighted
        inner_ref[0, n : n + 1, rows] = jnp.sum((weighted * pre).T, axis=0, keepdims=True)
        return jnp.sum(grad * pre * column(scale_ref[n : n + 1, rows]), axis=0, keepdims=True)

    def one(i, gain_grad):
        rows = pl.ds(pl.multiple_of(i * BLOCK, BLOCK), BLOCK)
        q = q_ref[rows, :]
        do = do_ref[rows, :]
        begin = begin_ref[0:1, rows]
        lse = lse_ref[0, 0:1, rows]
        delta = jnp.sum((do.astype(FULL) * o_ref[rows, :].astype(FULL)).T, axis=0, keepdims=True)
        at = lax.broadcasted_iota(jnp.int32, (BLOCK, BLOCK), 0)
        query_at = lax.broadcasted_iota(jnp.int32, (1, BLOCK), 1) + i * BLOCK

        def step(j, acc):
            keys = pl.ds(pl.multiple_of(j * BLOCK, BLOCK), BLOCK)
            s = dot_nt(k_ref[keys, :], q)
            key_at = at + j * BLOCK
            s = jnp.where((key_at >= begin) & (key_at <= query_at), s, NEG)
            p = jnp.exp2(s * factor - lse)
            dp = dot_nt(v_ref[keys, :], do)
            ds = (p * (dp - delta)).astype(LOW)
            dv_ref[keys, :] += dot(p.astype(LOW), do)
            dk_ref[keys, :] += dot(ds, q)
            return acc + dot(kt_ref[:, keys], ds)

        acc = lax.fori_loop(first_ref[i], i + 1, step, jnp.zeros((HEAD, BLOCK), FULL))
        return gain_grad + finish(rows, 0, acc.T * norm, qp_ref, gq_ref)

    gain_grad_ref[0:1, :] = lax.fori_loop(0, blocks, one, jnp.zeros((1, HEAD), FULL))

    def close(i, gain_grad):
        rows = pl.ds(pl.multiple_of(i * BLOCK, BLOCK), BLOCK)
        gv_ref[rows, :] = dv_ref[rows, :].astype(LOW)
        return gain_grad + finish(rows, 1, dk_ref[rows, :] * norm, kp_ref, gk_ref)

    gain_grad_ref[1:2, :] = lax.fori_loop(0, blocks, close, jnp.zeros((1, HEAD), FULL))


def attend_backward(q, k, v, out, grad, lse, pre, scales, gains, cosine, sine, first, begin):
    rows, wide = q.shape
    heads = wide // HEAD
    col = lambda shift: pl.BlockSpec((rows, HEAD), lambda h, f: (0, h + shift))
    fixed = lambda shape: pl.BlockSpec(shape, lambda h, f: (0,) * len(shape))
    pair = pl.BlockSpec((2, HEAD), lambda h, f: (0, h))
    full = jax.ShapeDtypeStruct((rows, wide), FULL)
    return pl.pallas_call(
        attend_backward_kernel,
        grid_spec=pltpu.PrefetchScalarGridSpec(
            num_scalar_prefetch=1,
            grid=(heads,),
            in_specs=[col(0)] * 5 + [pl.BlockSpec((1, 1, rows), lambda h, f: (h, 0, 0)), col(0), col(heads), fixed((2, rows)),
                      pair, fixed((rows, HEAD)), fixed((rows, HEAD)), fixed((1, rows))],
            out_specs=[col(0)] * 3 + [pl.BlockSpec((1, 2, rows), lambda h, f: (h, 0, 0)), pair],
            scratch_shapes=[pltpu.VMEM((HEAD, rows), LOW), pltpu.VMEM((rows, HEAD), FULL), pltpu.VMEM((rows, HEAD), FULL)],
        ),
        out_shape=[full, full, jax.ShapeDtypeStruct((rows, wide), LOW), jax.ShapeDtypeStruct((heads, 2, rows), FULL), jax.ShapeDtypeStruct((2, wide), FULL)],
        compiler_params=pltpu.CompilerParams(vmem_limit_bytes=48 * 2**20),
        cost_estimate=pl.CostEstimate(flops=heads * rows * rows * HEAD * 5, bytes_accessed=rows * wide * 40, transcendentals=heads * rows * rows // 2),
        name="attend_backward",
    )(first, q, k, v, out, grad, lse, pre, pre, scales, gains, cosine, sine, begin)


def per_device(
    tokens,
    cotangent,
    lengths,
    placement,
    w_query,
    w_key,
    w_value,
    w_output,
    query_gain,
    key_gain,
    attn_gain,
    w_gate,
    w_up,
    w_down,
    mlp_gain,
):
    data, seq = lax.axis_size("dp"), lax.axis_size("seq")
    seq_at = lax.axis_index("seq")
    _, count, width = tokens.shape
    row_len = count * seq
    own = width // seq
    row_ring = Ring([row_cycle(seq)])
    inputs = tokens.reshape(count, width)
    begin = layout(lengths, placement, row_len)
    first_block = begin[::BLOCK] // BLOCK
    cosine, sine = rope_tables(jnp.arange(row_len, dtype=jnp.int32) - begin)
    begin = begin[None]

    packed = jnp.stack([w_query, w_key, w_value], axis=1).reshape(-1, 3, seq, own)
    packed = jnp.moveaxis(packed, 2, 0).reshape(seq, -1, 3 * own)
    hid = w_gate.shape[1]
    chips = data_bits(data)[:-1]
    state = {"gains": jnp.stack([query_gain, key_gain, attn_gain, mlp_gain])[None]}
    gain_bits = bits_of(data * seq)

    def more_gains():
        if gain_bits:
            state["gains"] = gain_step(state["gains"], gain_bits.pop(0))
        return state["gains"]

    def beside(step):
        out = [more_gains()]
        if step == 1:
            state["down"] = swap_chips(w_down, chips)
            state["w_heads"] = lax.all_to_all(packed, "seq", split_axis=0, concat_axis=0, tiled=True)
            out.append(state["w_heads"])
        elif step == 2:
            state["w_heads"] = swap_chips(state["w_heads"].reshape(-1, 3 * own), chips)
            state["w_out"] = stack_output_weights(w_output)
            out += [state["w_heads"], state["w_out"], state["down"]]
        elif step == 3:
            state["w_heads"] = place_over_data(swap_cores(state["w_heads"]))
            state["gate"] = swap_chips(w_gate, chips)
            out += [state["w_heads"], state["gate"]]
        return out

    row_chunks = row_ring.gather(inputs, beside)
    w_heads = state["w_heads"]
    pre = jnp.zeros((row_len, 3 * own), FULL)
    row_tokens = jnp.zeros((row_len, width), LOW)
    last = row_ring.size // 2
    for offset, chunk in row_chunks.items():
        if offset == last:
            chunk, pre = after((chunk, pre))
        start = row_ring.owner(offset) * count
        pre = lax.dynamic_update_slice(pre, dot(chunk, w_heads), (start, 0))
        row_tokens = lax.dynamic_update_slice(row_tokens, chunk, (start, 0))
    while gain_bits:
        more_gains()
    gains = jnp.moveaxis(state["gains"], 0, 1).reshape(4, -1).astype(FULL)
    gain_attn, gain_mlp = gains[2], gains[3]
    gains_own = lax.dynamic_slice(gains, (0, seq_at * own), (2, own))
    state["up"] = swap_chips(after(w_up, row_chunks[last]), chips)

    query_pre, key_pre = pre[:, :own], pre[:, own : 2 * own]
    squares = jnp.stack([jnp.sum(query_pre * query_pre, axis=1), jnp.sum(key_pre * key_pre, axis=1)])
    scales = lax.rsqrt(sum_over(squares, "seq", seq) / width + EPSILON)
    attn_heads, query_rot, key_rot, values, log_sums = attend_forward(
        pre, scales, gains_own, cosine, sine, first_block, begin
    )
    w_out = gather_output_weights(after(state["w_out"], scales), row_ring)
    attn_tokens = lax.all_to_all(
        attn_heads.reshape(seq, count, own), "seq", split_axis=0, concat_axis=0, tiled=True
    )

    near = after([state[n] for n in ("gate", "up", "down")], attn_heads)
    near = [swap_cores(n) for n in near]
    gate_up = pack(near[0], near[1])
    down = jnp.concatenate([near[2][m] for m in range(data)], axis=1)
    attn_tokens = jnp.moveaxis(attn_tokens, 0, 1).reshape(count, width)
    attn_pre = dot(attn_tokens, w_out)
    attn_scale = rms_scale(attn_pre)
    middle = inputs.astype(FULL) + attn_pre * attn_scale * gain_attn
    middle_low = middle.astype(LOW)

    mids = row_ring.gather(swap_blocks(middle_low))
    saved = {}

    def mlp_part(offset):
        offset = offset if offset in mids else -offset
        both = dot(mids[offset], gate_up)
        gate, up = both[:, :hid], both[:, hid:]
        hidden = (gate * jax.nn.sigmoid(gate) * up).astype(LOW)
        saved[offset] = gate, up, hidden
        return dot(hidden, down)

    mlp_pre = swap_blocks(row_ring.scatter(mlp_part))
    mlp_scale = rms_scale(mlp_pre)
    layer_out = (middle + mlp_pre * mlp_scale * gain_mlp).astype(LOW).reshape(tokens.shape)
    grad_final = cotangent.reshape(count, width).astype(FULL)
    grad_mlp_pre, grad_gain_mlp = norm_back(grad_final, mlp_pre, mlp_scale, gain_mlp)
    grads = row_ring.gather(swap_blocks(grad_mlp_pre.astype(LOW)))
    grad_both = {}

    def middle_part(offset):
        offset = offset if offset in mids else -offset
        gate, up, hidden = saved[offset]
        grad_hidden = dot_nt(grads[offset], down)
        sig = jax.nn.sigmoid(gate)
        grad_gate = grad_hidden * up * sig * (1.0 + gate * (1.0 - sig))
        grad_up = grad_hidden * gate * sig
        both = jnp.concatenate([grad_gate.astype(LOW), grad_up.astype(LOW)], axis=1)
        grad_both[offset] = both
        return dot_nt(both, gate_up)

    grad_middle = grad_final + swap_blocks(row_ring.scatter(middle_part))
    order = list(mids)
    mid_rows = jnp.concatenate([mids[o] for o in order])
    grad_rows = jnp.concatenate([grads[o] for o in order])
    hidden = jnp.concatenate([saved[o][2] for o in order])
    both = jnp.concatenate([grad_both[o] for o in order])
    part_down = dot_tn(hidden, grad_rows).astype(LOW)
    grad_down = scatter_over_data(jnp.split(part_down, data, axis=1))
    grad_in = scatter_over_data(jnp.split(dot_tn(mid_rows, both).astype(LOW), data))
    grad_gate, grad_up = grad_in[:, :hid], grad_in[:, hid:]

    grad_attn_pre, grad_gain_attn = norm_back(grad_middle, attn_pre, attn_scale, gain_attn)
    grad_attn_low = grad_attn_pre.astype(LOW)
    grad_heads = dot_nt(grad_attn_low, w_out).astype(LOW).reshape(count, seq, own)
    grad_heads = lax.all_to_all(
        jnp.moveaxis(grad_heads, 1, 0), "seq", split_axis=0, concat_axis=0, tiled=True
    )
    grad_heads = grad_heads.reshape(row_len, own)
    grad_output = scatter_output_grad(dot_tn(attn_tokens, grad_attn_low), row_ring)
    weighted_q, weighted_k, grad_v, inner, gain_part = attend_backward(
        query_rot,
        key_rot,
        values,
        attn_heads,
        grad_heads,
        log_sums,
        pre,
        scales,
        gains_own,
        cosine,
        sine,
        first_block,
        begin,
    )
    inner = sum_over(jnp.sum(inner, axis=0), "seq", seq) * (scales**3) / width
    by_token = jnp.concatenate([scales, inner]).T
    grad_qp = by_token[:, 0:1] * weighted_q - by_token[:, 2:3] * query_pre
    grad_kp = by_token[:, 1:2] * weighted_k - by_token[:, 3:4] * key_pre
    grad_pre = jnp.concatenate([grad_qp.astype(LOW), grad_kp.astype(LOW), grad_v], axis=1)

    def token_part(offset):
        start = row_ring.owner(offset) * count
        return dot_nt(lax.dynamic_slice_in_dim(grad_pre, start, count, 0), w_heads)

    grad_tokens = (grad_middle + row_ring.scatter(token_part)).astype(LOW).reshape(tokens.shape)
    part = dot_tn(row_tokens, grad_pre).astype(LOW)
    part = [
        lax.dynamic_slice_in_dim(part, (lax.axis_index("dp") ^ m) * (width // data), width // data, 0)
        for m in range(data)
    ]
    part = scatter_over_data(part).astype(LOW)
    part = lax.all_to_all(
        part.reshape(seq, -1, 3 * own), "seq", split_axis=0, concat_axis=0, tiled=True
    ).astype(FULL)
    part = jnp.moveaxis(part.reshape(seq, -1, 3, own), 0, 2).reshape(-1, 3, width)

    placed = lax.dynamic_update_slice(jnp.zeros((2, width), FULL), gain_part, (0, seq_at * own))
    placed = jnp.concatenate([placed, grad_gain_attn[None], grad_gain_mlp[None]])
    for bit in bits_of(data * seq):
        placed = placed + swap_all(placed, bit)
    share = width // (data * seq)
    start = (lax.axis_index("dp") * seq + seq_at) * share
    gain_grads = lax.dynamic_slice(placed, (0, start), (4, share))

    return (
        layer_out,
        grad_tokens,
        part[:, 0],
        part[:, 1],
        part[:, 2],
        grad_output,
        gain_grads[0],
        gain_grads[1],
        gain_grads[2],
        grad_gate,
        grad_up,
        grad_down,
        gain_grads[3],
    )


def solution(mesh):
    rows = P("dp", "seq", None)
    both = P(("dp", "seq"), None)
    flat = P(("dp", "seq"))
    return jax.shard_map(
        per_device,
        mesh=mesh,
        in_specs=(rows, rows, P(), P())
        + (both,) * 4
        + (flat,) * 3
        + (P("dp", "seq"), P("dp", "seq"), P("seq", "dp"), flat),
        out_specs=(rows, rows)
        + (both,) * 4
        + (flat,) * 3
        + (P("dp", "seq"), P("dp", "seq"), P("seq", "dp"), flat),
        check_vma=False,
    )
```

```python
import math

import jax
import jax.numpy as jnp
from jax import lax
from jax.experimental import pallas as pl
from jax.experimental.pallas import tpu as pltpu
from jax.sharding import PartitionSpec as P

HEAD = 128
LEVELS = 4
EPSILON = 1e-06
ROPE_BASE = 500000.0
LOW = jnp.bfloat16
FULL = jnp.float32
NEG = -1e30
LOG2E = math.log2(math.e)
LIGHT = pl.CostEstimate(flops=1, bytes_accessed=1, transcendentals=0)
BLOCK = 512


def dot(left, right):
    return jnp.dot(left, right, preferred_element_type=FULL)


def dot_nt(left, right):
    return lax.dot_general(left, right, (((1,), (1,)), ((), ())), preferred_element_type=FULL)


def dot_tn(left, right):
    return lax.dot_general(left, right, (((0,), (0,)), ((), ())), preferred_element_type=FULL)


def swap(val, axis, mask):
    size = lax.axis_size(axis)
    return lax.ppermute(val, axis, [(i, i ^ mask) for i in range(size)])


def swap_all(val, mask):
    size = lax.axis_size("dp") * lax.axis_size("seq")
    return lax.ppermute(val, ("dp", "seq"), [(i, i ^ mask) for i in range(size)])


def tie(*vals):
    return lax.optimization_barrier(vals)


def bits_of(size):
    return [1 << i for i in range(size.bit_length() - 1)]


def sum_over(val, axis, size):
    for bit in bits_of(size):
        val = val + swap(val, axis, bit)
    return val


class Ring:
    def __init__(self, cycles):
        self.size = len(cycles[0])
        self.forth = [(c[i], c[(i + 1) % self.size]) for c in cycles for i in range(self.size)]
        self.back = [(b, a) for a, b in self.forth]
        total = self.size * len(cycles)
        owners = [[0] * self.size for _ in range(total)]
        for c in cycles:
            for i, dev in enumerate(c):
                for off in range(self.size):
                    owners[dev][off] = c[(i + off) % self.size]
        self.owners = owners

    def owner(self, offset):
        at = lax.axis_index("seq")
        found = jnp.int32(self.owners[0][offset % self.size])
        for dev, row in enumerate(self.owners[1:], 1):
            found = lax.select(at == dev, jnp.int32(row[offset % self.size]), found)
        return found

    def right(self, val):
        return lax.ppermute(val, "seq", self.forth)

    def left(self, val):
        return lax.ppermute(val, "seq", self.back)

    def gather(self, own, state=None, between=None):
        half = self.size // 2
        chunks = {0: own}
        r = l = own
        for k in range(1, half):
            names = between(k) if between else ()
            r, l = self.right(r), self.left(l)
            if names:
                r, l, *beside = tie(r, l, *(state[n] for n in names))
                state |= dict(zip(names, beside))
            chunks[-k], chunks[k] = r, l
        mid = own.shape[0] // 2
        chunks[half] = jnp.concatenate([self.right(r[:mid]), self.left(l[mid:])], axis=0)
        return chunks

    def scatter_steps(self, part, hold=lax.optimization_barrier):
        half = self.size // 2
        far = part(half).astype(LOW)
        mid = far.shape[0] // 2
        r, l = yield far[:mid], far[mid:]
        r, l = self.right(r), self.left(l)
        zero = jnp.zeros((), LOW)
        r = lax.pad(r, zero, ((0, mid, 0), (0, 0, 0)))
        l = lax.pad(l, zero, ((mid, 0, 0), (0, 0, 0)))
        for k in range(half - 1, 0, -1):
            a = hold(part(k)) + r.astype(FULL)
            b = hold(part(-k)) + l.astype(FULL)
            r, l = yield a.astype(LOW), b.astype(LOW)
            r, l = self.right(r), self.left(l)
        return hold(part(0)) + r.astype(FULL) + l.astype(FULL)

    def scatter(self, part, hook=None):
        return finish(self.scatter_steps(part), hook)


def finish(steps, hook=None, sent=None, step=0):
    try:
        sent = next(steps) if sent is None else sent
        while True:
            sent = steps.send(hook(step, sent) if hook else sent)
            step += 1
    except StopIteration as end:
        return end.value


def row_cycle(size):
    if size % LEVELS or size == LEVELS:
        return list(range(size))
    cols = size // LEVELS
    walk = [(0, 0)]
    for z in range(LEVELS):
        span = list(range(1, cols))
        walk += [(z, x) for x in (span if z % 2 == 0 else span[::-1])]
    walk += [(z, 0) for z in range(LEVELS - 1, 0, -1)]
    return [z * cols + x for z, x in walk]


def data_bits(size):
    return [b for b in bits_of(size) if b != 1] + [1]


def swap_chips(shard, bits):
    copies = {0: shard}
    for bit in bits:
        copies |= {mask ^ bit: swap(val, "dp", bit) for mask, val in copies.items()}
    return copies


def swap_cores(copies):
    return copies | {mask ^ 1: swap(val, "dp", 1) for mask, val in copies.items()}


def assemble_kernel(plan, at_ref, *refs):
    out_ref, sems = refs[-2], refs[-1]
    copies = []
    for i, (source, row, rows) in enumerate(plan):
        cols = refs[source].shape[1]
        place = (
            pl.ds(pl.multiple_of(at_ref[2 * i], 16), rows),
            pl.ds(pl.multiple_of(at_ref[2 * i + 1], 128), cols),
        )
        copies.append(
            pltpu.make_async_copy(refs[source].at[pl.ds(row, rows), :], out_ref.at[place], sems.at[i])
        )
    for copy in copies:
        copy.start()
    for copy in copies:
        copy.wait()


def assemble(shape, pieces):
    arrays, plan, at = [], [], []
    for val, row, rows, to_row, to_col in pieces:
        known = [i for i, a in enumerate(arrays) if a is val]
        if not known:
            arrays.append(val)
        plan.append((known[0] if known else len(arrays) - 1, row, rows))
        at += [to_row, to_col]
    at = jnp.stack([jnp.asarray(a, jnp.int32) for a in at])
    return pl.pallas_call(
        lambda at_ref, *refs: assemble_kernel(plan, at_ref, *refs),
        grid_spec=pltpu.PrefetchScalarGridSpec(
            num_scalar_prefetch=1,
            grid=(1,),
            in_specs=[pl.BlockSpec(memory_space=pl.ANY)] * len(arrays),
            out_specs=pl.BlockSpec(shape, lambda i, at: (0, 0)),
            scratch_shapes=[pltpu.SemaphoreType.DMA((len(plan),))],
        ),
        out_shape=jax.ShapeDtypeStruct(shape, LOW),
        compiler_params=pltpu.CompilerParams(vmem_limit_bytes=40 * 2**20),
        cost_estimate=pl.CostEstimate(flops=0, bytes_accessed=4 * shape[0] * shape[1], transcendentals=0),
        name="assemble",
    )(at, *arrays)


def place_over_data(copies, axis=0, shift=0):
    me = lax.axis_index("dp")
    pieces = []
    for mask, val in copies.items():
        at = [shift, shift]
        at[axis] = (me ^ mask) * val.shape[axis]
        pieces.append((val, 0, val.shape[0], at[0], at[1]))
    return pieces


def blocks_over_data(val, axis):
    size = lax.axis_size("dp")
    part = val.shape[axis] // size
    return [
        lax.dynamic_slice_in_dim(val, (lax.axis_index("dp") ^ m) * part, part, axis) for m in range(size)
    ]


def scatter_over_data(blocks):
    order = data_bits(len(blocks))[::-1]
    blocks = dict(enumerate(blocks))
    for bit in order[:-1]:
        out = {}
        for m in [m for m in blocks if not m & bit]:
            out[m] = (blocks[m].astype(FULL) + swap(blocks[m ^ bit], "dp", bit).astype(FULL)).astype(LOW)
        blocks = out
    return blocks[0], blocks[order[-1]]


def last_over_data(sent):
    return swap(sent, "dp", data_bits(lax.axis_size("dp"))[0])


def gain_step(val, bit):
    me = lax.axis_index("dp") * lax.axis_size("seq") + lax.axis_index("seq")
    got = swap_all(val, bit)
    upper = (me // bit) % 2 == 1
    return jnp.concatenate([jnp.where(upper, got, val), jnp.where(upper, val, got)], axis=0)


def gather_output_weights(row_ring, state, between, chips):
    seq = lax.axis_size("seq")
    me = lax.axis_index("dp")
    rows, width = state["w_out"].shape
    chunks = row_ring.gather(state["w_out"], state, between)
    half = row_ring.size // 2
    groups = [[0, 1, -1]] + [[k, -k] for k in range(2, half)] + [[half]]
    pieces = []
    for group in groups:
        val = jnp.concatenate([chunks[o] for o in group])
        for mask, block in swap_cores(swap_chips(val, chips)).items():
            for i, o in enumerate(group):
                to = ((me ^ mask) * seq + row_ring.owner(o)) * rows
                pieces.append((block, i * rows, rows, to, 0))
    return assemble((width, width), pieces)


def output_grad_steps(part, row_ring):
    data, seq = lax.axis_size("dp"), lax.axis_size("seq")
    me = lax.axis_index("dp")
    tall = data // 2
    width = part.shape[1]
    rows = part.shape[0] // (data * seq)
    part = part.reshape(tall, 2, seq, rows, width)
    kept = lax.dynamic_index_in_dim(part, me % 2, 1, False)
    sent = lax.dynamic_index_in_dim(part, 1 - me % 2, 1, False)
    kept = (kept.astype(FULL) + swap(sent, "dp", 1).astype(FULL)).astype(LOW)

    def block(offset):
        one = lax.dynamic_index_in_dim(kept, row_ring.owner(offset), 1, False)
        return one.reshape(tall * rows, width).astype(FULL)

    return row_ring.scatter_steps(block, lambda val: val)


def finish_output_grad(val):
    data = lax.axis_size("dp")
    me = lax.axis_index("dp")
    val = val.reshape(data // 2, -1, val.shape[1])
    _, rows, width = val.shape
    for bit in data_bits(data)[:-1][::-1]:
        upper = (me // bit) % 2
        val = val.reshape(2, val.shape[0] // 2, rows, width)
        kept = lax.dynamic_index_in_dim(val, upper, 0, False)
        sent = lax.dynamic_index_in_dim(val, 1 - upper, 0, False)
        val = kept + swap(sent, "dp", bit)
    return val.reshape(rows, width)


def rms_scale(vals):
    return lax.rsqrt(jnp.mean(vals * vals, axis=-1, keepdims=True) + EPSILON)


def norm_back(grad_out, pre, scale, gain):
    weighted = grad_out * gain
    inner = jnp.mean(weighted * pre, axis=-1, keepdims=True)
    grad_pre = scale * weighted - pre * (scale * scale * scale) * inner
    grad_gain = jnp.sum(grad_out * pre * scale, axis=0)
    return (grad_pre, grad_gain)


def rope_tables(positions):
    half = HEAD // 2
    freq = ROPE_BASE ** (-2.0 * jnp.arange(half, dtype=FULL) / HEAD)
    angle = positions.astype(FULL)[:, None] * freq[None, :]
    cosine, sine = jnp.cos(angle), jnp.sin(angle)
    return jnp.concatenate([cosine, cosine], 1), jnp.concatenate([-sine, sine], 1)


def layout(lengths, placement, row_len):
    stored, docs = lengths.shape
    rows = jnp.arange(placement.shape[0], dtype=jnp.int32)
    row = jnp.sum(jnp.where(rows == lax.axis_index("dp"), placement, 0))
    doc_lens = jnp.sum(
        jnp.where(jnp.arange(stored, dtype=jnp.int32)[:, None] == row, lengths, 0), axis=0
    )
    upto = jnp.arange(docs, dtype=jnp.int32)
    doc_ends = jnp.sum(jnp.where(upto[None, :] <= upto[:, None], doc_lens[None, :], 0), axis=1)
    at = jnp.arange(row_len, dtype=jnp.int32)
    passed = at[:, None] >= doc_ends[None, :]
    return jnp.max(jnp.where(passed, doc_ends[None, :], 0), axis=1)


def column(row):
    return jnp.broadcast_to(row, (HEAD, row.shape[1])).T

def attend_forward_kernel(first_ref, q_ref, k_ref, v_ref, scale_ref, gain_ref, cos_ref, sin_ref, begin_ref,
                          out_ref, qr_ref, kr_ref, vl_ref, lse_ref, vt_ref):
    blocks = q_ref.shape[0] // BLOCK
    factor = HEAD ** -0.5 * LOG2E

    def prepare(i, _):
        rows = pl.ds(pl.multiple_of(i * BLOCK, BLOCK), BLOCK)
        for n, (src, dst) in enumerate(((q_ref, qr_ref), (k_ref, kr_ref))):
            x = src[rows, :] * column(scale_ref[n : n + 1, rows]) * gain_ref[n : n + 1, :]
            x = x * cos_ref[rows, :] + pltpu.roll(x, HEAD // 2, 1) * sin_ref[rows, :]
            dst[rows, :] = x.astype(LOW)
        v = v_ref[rows, :].astype(LOW)
        vl_ref[rows, :] = v
        vt_ref[:, rows] = v.T
        return 0

    lax.fori_loop(0, blocks, prepare, 0)

    def one(i, _):
        rows = pl.ds(pl.multiple_of(i * BLOCK, BLOCK), BLOCK)
        q = qr_ref[rows, :]
        begin = begin_ref[0:1, rows]
        at = lax.broadcasted_iota(jnp.int32, (BLOCK, BLOCK), 0)
        query_at = lax.broadcasted_iota(jnp.int32, (1, BLOCK), 1) + i * BLOCK

        def step(j, carry):
            top, total, acc = carry
            keys = pl.ds(pl.multiple_of(j * BLOCK, BLOCK), BLOCK)
            s = dot_nt(kr_ref[keys, :], q)
            key_at = at + j * BLOCK
            s = jnp.where((key_at >= begin) & (key_at <= query_at), s, NEG)
            new = jnp.maximum(top, jnp.max(s, axis=0, keepdims=True))
            p = jnp.exp2((s - new) * factor)
            shrink = jnp.exp2((top - new) * factor)
            total = total * shrink + jnp.sum(p, axis=0, keepdims=True)
            acc = acc * shrink + dot(vt_ref[:, keys], p.astype(LOW))
            return new, total, acc

        start = (jnp.full((1, BLOCK), NEG, FULL), jnp.zeros((1, BLOCK), FULL), jnp.zeros((HEAD, BLOCK), FULL))
        top, total, acc = lax.fori_loop(first_ref[i], i + 1, step, start)
        out_ref[rows, :] = (acc / total).T.astype(LOW)
        lse_ref[0, 0:1, rows] = top * factor + jnp.log2(total)
        return 0

    lax.fori_loop(0, blocks, one, 0)


def attend_forward(pre, scales, gains, cosine, sine, first, begin):
    rows, wide = pre.shape
    heads = wide // (3 * HEAD)

    def col(shift):
        return pl.BlockSpec((rows, HEAD), lambda h, f: (0, h + shift))

    def fixed(*shape):
        return pl.BlockSpec(shape, lambda h, f: (0,) * len(shape))

    return pl.pallas_call(
        attend_forward_kernel,
        grid_spec=pltpu.PrefetchScalarGridSpec(
            num_scalar_prefetch=1,
            grid=(heads,),
            in_specs=[
                col(0),
                col(heads),
                col(2 * heads),
                fixed(2, rows),
                pl.BlockSpec((2, HEAD), lambda h, f: (0, h)),
                fixed(rows, HEAD),
                fixed(rows, HEAD),
                fixed(1, rows),
            ],
            out_specs=[col(0)] * 4 + [pl.BlockSpec((1, 1, rows), lambda h, f: (h, 0, 0))],
            scratch_shapes=[pltpu.VMEM((HEAD, rows), LOW)],
        ),
        out_shape=[jax.ShapeDtypeStruct((rows, heads * HEAD), LOW)] * 4
        + [jax.ShapeDtypeStruct((heads, 1, rows), FULL)],
        compiler_params=pltpu.CompilerParams(vmem_limit_bytes=48 * 2**20),
        cost_estimate=LIGHT,
        name="attend_forward",
    )(first, pre, pre, pre, scales, gains, cosine, sine, begin)


def attend_backward_kernel(first_ref, q_ref, k_ref, v_ref, o_ref, do_ref, lse_ref, qp_ref, kp_ref, scale_ref, gain_ref, cos_ref, sin_ref, begin_ref,
                           gq_ref, gk_ref, gv_ref, inner_ref, gain_grad_ref, kt_ref, dk_ref, dv_ref):
    blocks = q_ref.shape[0] // BLOCK
    norm = HEAD ** -0.5
    factor = norm * LOG2E

    def prepare(i, _):
        rows = pl.ds(pl.multiple_of(i * BLOCK, BLOCK), BLOCK)
        kt_ref[:, rows] = k_ref[rows, :].T
        dk_ref[rows, :] = jnp.zeros((BLOCK, HEAD), FULL)
        dv_ref[rows, :] = jnp.zeros((BLOCK, HEAD), FULL)
        return 0

    lax.fori_loop(0, blocks, prepare, 0)

    def finish(rows, n, grad, pre_ref, out):
        grad = grad.astype(LOW).astype(FULL)
        grad = grad * cos_ref[rows, :] - pltpu.roll(grad, HEAD // 2, 1) * sin_ref[rows, :]
        weighted = grad * gain_ref[n : n + 1, :]
        pre = pre_ref[rows, :]
        out[rows, :] = weighted
        inner_ref[0, n : n + 1, rows] = jnp.sum((weighted * pre).T, axis=0, keepdims=True)
        return jnp.sum(grad * pre * column(scale_ref[n : n + 1, rows]), axis=0, keepdims=True)

    def one(i, gain_grad):
        rows = pl.ds(pl.multiple_of(i * BLOCK, BLOCK), BLOCK)
        q = q_ref[rows, :]
        do = do_ref[rows, :]
        begin = begin_ref[0:1, rows]
        lse = lse_ref[0, 0:1, rows]
        delta = jnp.sum((do.astype(FULL) * o_ref[rows, :].astype(FULL)).T, axis=0, keepdims=True)
        at = lax.broadcasted_iota(jnp.int32, (BLOCK, BLOCK), 0)
        query_at = lax.broadcasted_iota(jnp.int32, (1, BLOCK), 1) + i * BLOCK

        def step(j, acc):
            keys = pl.ds(pl.multiple_of(j * BLOCK, BLOCK), BLOCK)
            s = dot_nt(k_ref[keys, :], q)
            key_at = at + j * BLOCK
            s = jnp.where((key_at >= begin) & (key_at <= query_at), s, NEG)
            p = jnp.exp2(s * factor - lse)
            dp = dot_nt(v_ref[keys, :], do)
            ds = (p * (dp - delta)).astype(LOW)
            dv_ref[keys, :] += dot(p.astype(LOW), do)
            dk_ref[keys, :] += dot(ds, q)
            return acc + dot(kt_ref[:, keys], ds)

        acc = lax.fori_loop(first_ref[i], i + 1, step, jnp.zeros((HEAD, BLOCK), FULL))
        return gain_grad + finish(rows, 0, acc.T * norm, qp_ref, gq_ref)

    gain_grad_ref[0:1, :] = lax.fori_loop(0, blocks, one, jnp.zeros((1, HEAD), FULL))

    def close(i, gain_grad):
        rows = pl.ds(pl.multiple_of(i * BLOCK, BLOCK), BLOCK)
        gv_ref[rows, :] = dv_ref[rows, :].astype(LOW)
        return gain_grad + finish(rows, 1, dk_ref[rows, :] * norm, kp_ref, gk_ref)

    gain_grad_ref[1:2, :] = lax.fori_loop(0, blocks, close, jnp.zeros((1, HEAD), FULL))


def attend_backward(head, q, k, v, out, grad, lse, pre, scales, gains, cosine, sine, first, begin):
    rows = q.shape[0]
    heads = pre.shape[1] // (3 * HEAD)

    def col(shift):
        return pl.BlockSpec((rows, HEAD), lambda i, f: (0, shift))

    def fixed(*shape):
        return pl.BlockSpec(shape, lambda i, f: (0,) * len(shape))

    full = jax.ShapeDtypeStruct((rows, HEAD), FULL)
    return pl.pallas_call(
        attend_backward_kernel,
        grid_spec=pltpu.PrefetchScalarGridSpec(
            num_scalar_prefetch=1,
            grid=(1,),
            in_specs=[col(head)] * 5
            + [
                pl.BlockSpec((1, 1, rows), lambda i, f: (head, 0, 0)),
                col(head),
                col(heads + head),
                fixed(2, rows),
                pl.BlockSpec((2, HEAD), lambda i, f: (0, head)),
                fixed(rows, HEAD),
                fixed(rows, HEAD),
                fixed(1, rows),
            ],
            out_specs=[fixed(rows, HEAD)] * 3 + [fixed(1, 2, rows), fixed(2, HEAD)],
            scratch_shapes=[
                pltpu.VMEM((HEAD, rows), LOW),
                pltpu.VMEM((rows, HEAD), FULL),
                pltpu.VMEM((rows, HEAD), FULL),
            ],
        ),
        out_shape=[
            full,
            full,
            jax.ShapeDtypeStruct((rows, HEAD), LOW),
            jax.ShapeDtypeStruct((1, 2, rows), FULL),
            jax.ShapeDtypeStruct((2, HEAD), FULL),
        ],
        compiler_params=pltpu.CompilerParams(vmem_limit_bytes=48 * 2**20),
        cost_estimate=LIGHT,
        name="attend_backward",
    )(first, q, k, v, out, grad, lse, pre, pre, scales, gains, cosine, sine, begin)


def per_device(
    tokens,
    cotangent,
    lengths,
    placement,
    w_query,
    w_key,
    w_value,
    w_output,
    query_gain,
    key_gain,
    attn_gain,
    w_gate,
    w_up,
    w_down,
    mlp_gain,
):
    data, seq = lax.axis_size("dp"), lax.axis_size("seq")
    seq_at = lax.axis_index("seq")
    _, count, width = tokens.shape
    row_len = count * seq
    own = width // seq
    row_ring = Ring([row_cycle(seq)])
    inputs = tokens.reshape(count, width)
    begin = layout(lengths, placement, row_len)

    packed = jnp.stack([w_query, w_key, w_value], axis=1).reshape(-1, 3, seq, own)
    packed = jnp.moveaxis(packed, 2, 0).reshape(seq, -1, 3 * own)
    hid = w_gate.shape[1]
    chips = data_bits(data)[:-1]
    state = {"gains": jnp.stack([query_gain, key_gain, attn_gain, mlp_gain])[None]}
    gain_bits = bits_of(data * seq)

    def more_gains():
        if gain_bits:
            state["gains"] = gain_step(state["gains"], gain_bits.pop(0))

    def beside(step):
        more_gains()
        if step == 1:
            state["down"] = swap_chips(w_down, chips)
            state["w_heads"] = lax.all_to_all(packed, "seq", split_axis=0, concat_axis=0, tiled=True)
            return ["gains"]
        if step == 2:
            state["gate"] = swap_chips(w_gate, chips)
            return ["gains", "w_heads", "down", "gate", "begin"]
        if step == 3:
            state["w_heads"] = swap_chips(state["w_heads"].reshape(-1, 3 * own), chips)
            state["w_out"], state["up"] = w_output, w_up
            return ["gains", "w_heads", "w_out", "up"]
        return ["gains"]

    state["begin"] = begin
    row_chunks = row_ring.gather(inputs, state, beside)
    begin = state["begin"]
    first_block = begin[::BLOCK] // BLOCK
    cosine, sine = rope_tables(jnp.arange(row_len, dtype=jnp.int32) - begin)
    begin = begin[None]
    state["up"] = swap_chips(state["up"], chips)
    w_heads = assemble((width, 3 * own), place_over_data(swap_cores(state["w_heads"])))
    row_tokens = jnp.zeros((row_len, width), LOW)
    for offset, chunk in row_chunks.items():
        row_tokens = lax.dynamic_update_slice(row_tokens, chunk, (row_ring.owner(offset) * count, 0))
    pre = dot(row_tokens, w_heads)
    while gain_bits:
        more_gains()
    gains = jnp.moveaxis(state["gains"], 0, 1).reshape(4, -1).astype(FULL)
    gain_attn, gain_mlp = gains[2], gains[3]
    gains_own = lax.dynamic_slice(gains, (0, seq_at * own), (2, own))
    query_pre, key_pre = pre[:, :own], pre[:, own : 2 * own]
    squares = jnp.stack([jnp.sum(query_pre * query_pre, axis=1), jnp.sum(key_pre * key_pre, axis=1)])
    scales = lax.rsqrt(sum_over(squares, "seq", seq) / width + EPSILON)
    state["scales"] = scales

    def beside_output(step):
        if step == 3:
            state["attn"] = attend_forward(
                pre, state["scales"], gains_own, cosine, sine, first_block, begin
            )
            return ["attn"]
        return ["scales", "up"] if step == 2 else []

    w_out = gather_output_weights(row_ring, state, beside_output, chips)
    scales = state["scales"]
    attn_heads, query_rot, key_rot, values, log_sums = state["attn"]
    attn_tokens = lax.all_to_all(
        attn_heads.reshape(seq, count, own), "seq", split_axis=0, concat_axis=0, tiled=True
    )
    attn_tokens = jnp.moveaxis(attn_tokens, 0, 1).reshape(count, width)

    near, attn_rows = tie([state[n] for n in ("gate", "up", "down")], attn_tokens)
    near = [swap_cores(n) for n in near]
    gate_up = assemble((width, 2 * hid), place_over_data(near[0]) + place_over_data(near[1], 0, hid))
    down = assemble((hid, width), place_over_data(near[2], 1))
    attn_pre = dot(attn_tokens, w_out)
    attn_scale = rms_scale(attn_pre)
    middle = inputs.astype(FULL) + attn_pre * attn_scale * gain_attn
    middle_low = middle.astype(LOW)

    mids = row_ring.gather(middle_low)
    saved = {}

    def mlp_part(offset):
        offset = offset if offset in mids else -offset
        both = dot(mids[offset], gate_up)
        gate, up = both[:, :hid], both[:, hid:]
        hidden = (gate * jax.nn.sigmoid(gate) * up).astype(LOW)
        saved[offset] = gate, up, hidden
        return dot(hidden, down)

    mlp_pre = row_ring.scatter(mlp_part)
    mlp_scale = rms_scale(mlp_pre)
    layer_out = (middle + mlp_pre * mlp_scale * gain_mlp).astype(LOW).reshape(tokens.shape)
    grad_final = cotangent.reshape(count, width).astype(FULL)
    grad_mlp_pre, grad_gain_mlp = norm_back(grad_final, mlp_pre, mlp_scale, gain_mlp)
    grads = row_ring.gather(grad_mlp_pre.astype(LOW))
    grad_both = {}

    def middle_part(offset):
        gate, up, hidden = saved[offset]
        grad_hidden = dot_nt(grads[offset], down)
        sig = jax.nn.sigmoid(gate)
        grad_gate = grad_hidden * up * sig * (1.0 + gate * (1.0 - sig))
        grad_up = grad_hidden * gate * sig
        grad_both[offset] = grad_gate.astype(LOW), grad_up.astype(LOW)
        return dot_nt(jnp.concatenate(grad_both[offset], axis=1), gate_up)

    order = list(mids)
    ffn = {"mids": jnp.concatenate([mids[o] for o in order])}
    ffn["grads"] = jnp.concatenate([grads[o] for o in order])
    ffn["hidden"] = jnp.concatenate([saved[o][2] for o in order])

    half = row_ring.size // 2

    def beside_middle(step, sent):
        if step == half - 2:
            ffn["down"] = dot_tn(ffn["hidden"], ffn["grads"]).astype(LOW)
            sent, ffn["down"] = tie(sent, ffn["down"])
        if step == half - 1:
            rows = jnp.concatenate([grad_both[o][0] for o in order])
            ffn["gate"] = dot_tn(ffn["mids"], rows).astype(LOW)
            sent, ffn["gate"], ffn["down"] = tie(sent, ffn["gate"], ffn["down"])
        return sent

    middle_parts = {o: middle_part(o) for o in order}
    grad_middle = row_ring.scatter(lambda o: middle_parts[o], beside_middle)
    rows = jnp.concatenate([grad_both[o][1] for o in order])
    ffn["up"] = dot_tn(ffn["mids"], rows).astype(LOW)
    sums = {n: scatter_over_data(blocks_over_data(ffn[n], a)) for n, a in (("down", 1), ("gate", 0))}
    grad_middle, sums, ffn["up"] = tie(grad_middle, sums, ffn["up"])
    grad_middle = grad_final + grad_middle

    grad_attn_pre, grad_gain_attn = norm_back(grad_middle, attn_pre, attn_scale, gain_attn)
    grad_attn_low = grad_attn_pre.astype(LOW)
    grad_heads = dot_nt(grad_attn_low, w_out).astype(LOW)
    grad_heads, grad_attn_low = tie(grad_heads, grad_attn_low)
    grad_heads = jnp.moveaxis(grad_heads.reshape(count, seq, own), 1, 0)
    grad_heads = lax.all_to_all(grad_heads, "seq", split_axis=0, concat_axis=0, tiled=True)
    grad_heads = grad_heads.reshape(row_len, own)
    steps = output_grad_steps(dot_tn(attn_rows, grad_attn_low).astype(LOW), row_ring)
    sent = next(steps)
    sums["up"] = scatter_over_data(blocks_over_data(ffn["up"], 0))
    got = {n: last_over_data(sums[n][1]) for n in ("down", "gate")}
    grad_heads, sent, sums["up"] = tie(grad_heads, sent, sums["up"])
    got["up"] = last_over_data(sums["up"][1])
    sums = {n: val[0] for n, val in sums.items()}
    heads = []
    for head in range(own // HEAD):
        if head:
            sent = steps.send(sent)
            grad_heads, sent, *early = tie(grad_heads, sent, got["down"], got["gate"])
            got["down"], got["gate"] = early
        done = attend_backward(
            head,
            query_rot,
            key_rot,
            values,
            attn_heads,
            grad_heads,
            log_sums,
            pre,
            scales,
            gains_own,
            cosine,
            sine,
            first_block,
            begin,
        )
        heads.append(list(done))
    sent = steps.send(sent)
    weighted_q, weighted_k, grad_v = (
        jnp.concatenate([h[i] for h in heads], axis=1) for i in range(3)
    )
    inner = sum(h[3][0] for h in heads)
    inner, sent, got["up"] = tie(inner, sent, got["up"])
    gain_part = jnp.concatenate([h[4] for h in heads], axis=1)
    gain_part = lax.dynamic_update_slice(jnp.zeros((2, width), FULL), gain_part, (0, seq_at * own))
    inner = jnp.concatenate([inner, jnp.zeros((2, width - row_len), FULL)], axis=1)
    small = jnp.concatenate([inner, gain_part, grad_gain_attn[None], grad_gain_mlp[None]])
    small = sum_over(small, "seq", seq)
    inner, gain_sums = small[:2, :row_len], small[2:]
    last_sent = steps.send(sent)
    inner = inner * (scales**3) / width
    by_token = jnp.concatenate([scales, inner]).T
    grad_qp = by_token[:, 0:1] * weighted_q - by_token[:, 2:3] * query_pre
    grad_kp = by_token[:, 1:2] * weighted_k - by_token[:, 3:4] * key_pre
    grad_pre = jnp.concatenate([grad_qp.astype(LOW), grad_kp.astype(LOW), grad_v], axis=1)

    rest = {"pre": grad_pre, "output": last_sent, "sums": sums, "got": got}

    token_parts = dot_nt(grad_pre, w_heads).astype(LOW)

    def token_part(offset):
        start = row_ring.owner(offset) * count
        return lax.dynamic_slice_in_dim(token_parts, start, count, 0).astype(FULL)

    def beside_tokens(step, sent):
        names = ["pre"]
        if step == 1:
            names += ["sums", "got", "output"]
        if step == 2:
            rest["part"] = dot_tn(row_tokens, rest["pre"]).astype(LOW)
            names += ["part"]
        if step == 3:
            rest["part"] = scatter_over_data(blocks_over_data(rest["part"], 0))
            rest["part"] = rest["part"][0], last_over_data(rest["part"][1])
            names += ["part"]
        sent, *tied = tie(sent, *(rest[n] for n in names))
        rest.update(zip(names, tied))
        return sent

    grad_tokens = grad_middle + finish(
        row_ring.scatter_steps(token_part, lambda val: val), beside_tokens
    )
    grad_tokens = grad_tokens.astype(LOW).reshape(tokens.shape)
    gain_sums = sum_over(gain_sums, "dp", data)
    share = width // (data * seq)
    start = (lax.axis_index("dp") * seq + seq_at) * share
    gain_grads = lax.dynamic_slice(gain_sums, (0, start), (4, share))
    part = (rest["part"][0].astype(FULL) + rest["part"][1].astype(FULL)).astype(LOW)
    part = lax.all_to_all(
        part.reshape(seq, -1, 3 * own), "seq", split_axis=0, concat_axis=0, tiled=True
    ).astype(FULL)
    part = jnp.moveaxis(part.reshape(seq, -1, 3, own), 0, 2).reshape(-1, 3, width)
    sums, got = rest["sums"], rest["got"]
    grad_output = finish_output_grad(finish(steps, sent=rest["output"]))
    grad_down, grad_gate, grad_up = (
        sums[n].astype(FULL) + got[n].astype(FULL) for n in ("down", "gate", "up")
    )

    return (
        layer_out,
        grad_tokens,
        part[:, 0],
        part[:, 1],
        part[:, 2],
        grad_output,
        gain_grads[0],
        gain_grads[1],
        gain_grads[2],
        grad_gate,
        grad_up,
        grad_down,
        gain_grads[3],
    )


def solution(mesh):
    rows = P("dp", "seq", None)
    both = P(("dp", "seq"), None)
    flat = P(("dp", "seq"))
    return jax.shard_map(
        per_device,
        mesh=mesh,
        in_specs=(rows, rows, P(), P())
        + (both,) * 4
        + (flat,) * 3
        + (P("dp", "seq"), P("dp", "seq"), P("seq", "dp"), flat),
        out_specs=(rows, rows)
        + (both,) * 4
        + (flat,) * 3
        + (P("dp", "seq"), P("dp", "seq"), P("seq", "dp"), flat),
        check_vma=False,
    )
```

```python
import math

import jax
import jax.numpy as jnp
from jax import lax
from jax.experimental import pallas as pl
from jax.experimental.pallas import tpu as pltpu
from jax.sharding import PartitionSpec as P

HEAD = 128
LEVELS = 4
EPSILON = 1e-06
ROPE_BASE = 500000.0
LOW = jnp.bfloat16
FULL = jnp.float32
NEG = -1e30
LOG2E = math.log2(math.e)
LIGHT = pl.CostEstimate(flops=1, bytes_accessed=1, transcendentals=0)
BLOCK = 512


def dot(left, right):
    return jnp.dot(left, right, preferred_element_type=FULL)


def dot_nt(left, right):
    return lax.dot_general(left, right, (((1,), (1,)), ((), ())), preferred_element_type=FULL)


def dot_tn(left, right):
    return lax.dot_general(left, right, (((0,), (0,)), ((), ())), preferred_element_type=FULL)


def swap(val, axis, mask):
    size = lax.axis_size(axis)
    return lax.ppermute(val, axis, [(i, i ^ mask) for i in range(size)])


def swap_all(val, mask):
    size = lax.axis_size("dp") * lax.axis_size("seq")
    return lax.ppermute(val, ("dp", "seq"), [(i, i ^ mask) for i in range(size)])


def tie(*vals):
    return lax.optimization_barrier(vals)


def bits_of(size):
    return [1 << i for i in range(size.bit_length() - 1)]


def sum_over(val, axis, size):
    for bit in bits_of(size):
        val = val + swap(val, axis, bit)
    return val


class Ring:
    def __init__(self, cycles):
        self.size = len(cycles[0])
        self.forth = [(c[i], c[(i + 1) % self.size]) for c in cycles for i in range(self.size)]
        self.back = [(b, a) for a, b in self.forth]
        total = self.size * len(cycles)
        owners = [[0] * self.size for _ in range(total)]
        for c in cycles:
            for i, dev in enumerate(c):
                for off in range(self.size):
                    owners[dev][off] = c[(i + off) % self.size]
        self.owners = owners

    def owner(self, offset):
        at = lax.axis_index("seq")
        found = jnp.int32(self.owners[0][offset % self.size])
        for dev, row in enumerate(self.owners[1:], 1):
            found = lax.select(at == dev, jnp.int32(row[offset % self.size]), found)
        return found

    def right(self, val):
        return lax.ppermute(val, "seq", self.forth)

    def left(self, val):
        return lax.ppermute(val, "seq", self.back)

    def gather(self, own, state=None, between=None):
        half = self.size // 2
        chunks = {0: own}
        r = l = own
        for k in range(1, half):
            r, l = self.right(r), self.left(l)
            chunks[-k], chunks[k] = r, l
            names = between(k, chunks) if between else ()
            if names:
                r, l, *beside = tie(r, l, *(state[n] for n in names))
                state |= dict(zip(names, beside))
        mid = own.shape[0] // 2
        chunks[half] = jnp.concatenate([self.right(r[:mid]), self.left(l[mid:])], axis=0)
        return chunks

    def scatter_steps(self, part, hold=lax.optimization_barrier):
        half = self.size // 2
        far = part(half).astype(LOW)
        mid = far.shape[0] // 2
        r, l = yield far[:mid], far[mid:]
        r, l = self.right(r), self.left(l)
        zero = jnp.zeros((), LOW)
        r = lax.pad(r, zero, ((0, mid, 0), (0, 0, 0)))
        l = lax.pad(l, zero, ((mid, 0, 0), (0, 0, 0)))
        for k in range(half - 1, 0, -1):
            a = hold(part(k)) + r.astype(FULL)
            b = hold(part(-k)) + l.astype(FULL)
            r, l = yield a.astype(LOW), b.astype(LOW)
            r, l = self.right(r), self.left(l)
        return hold(part(0)) + r.astype(FULL) + l.astype(FULL)

    def scatter(self, part, hook=None):
        return finish(self.scatter_steps(part), hook)


def finish(steps, hook=None, sent=None, step=0):
    try:
        sent = next(steps) if sent is None else sent
        while True:
            sent = steps.send(hook(step, sent) if hook else sent)
            step += 1
    except StopIteration as end:
        return end.value


def row_cycle(size):
    if size % LEVELS or size == LEVELS:
        return list(range(size))
    cols = size // LEVELS
    walk = [(0, 0)]
    for z in range(LEVELS):
        span = list(range(1, cols))
        walk += [(z, x) for x in (span if z % 2 == 0 else span[::-1])]
    walk += [(z, 0) for z in range(LEVELS - 1, 0, -1)]
    return [z * cols + x for z, x in walk]


def data_bits(size):
    return [b for b in bits_of(size) if b != 1] + [1]


def swap_chips(shard, bits):
    copies = {0: shard}
    for bit in bits:
        copies |= {mask ^ bit: swap(val, "dp", bit) for mask, val in copies.items()}
    return copies


def swap_cores(copies):
    return copies | {mask ^ 1: swap(val, "dp", 1) for mask, val in copies.items()}


def assemble_kernel(plan, at_ref, *refs):
    out_ref, sems = refs[-2], refs[-1]
    copies = []
    for i, (source, row, rows) in enumerate(plan):
        cols = refs[source].shape[1]
        place = (
            pl.ds(pl.multiple_of(at_ref[2 * i], 16), rows),
            pl.ds(pl.multiple_of(at_ref[2 * i + 1], 128), cols),
        )
        copies.append(
            pltpu.make_async_copy(refs[source].at[pl.ds(row, rows), :], out_ref.at[place], sems.at[i])
        )
    for copy in copies:
        copy.start()
    for copy in copies:
        copy.wait()


def assemble(shape, pieces):
    arrays, plan, at = [], [], []
    for val, row, rows, to_row, to_col in pieces:
        known = [i for i, a in enumerate(arrays) if a is val]
        if not known:
            arrays.append(val)
        plan.append((known[0] if known else len(arrays) - 1, row, rows))
        at += [to_row, to_col]
    at = jnp.stack([jnp.asarray(a, jnp.int32) for a in at])
    return pl.pallas_call(
        lambda at_ref, *refs: assemble_kernel(plan, at_ref, *refs),
        grid_spec=pltpu.PrefetchScalarGridSpec(
            num_scalar_prefetch=1,
            grid=(1,),
            in_specs=[pl.BlockSpec(memory_space=pl.ANY)] * len(arrays),
            out_specs=pl.BlockSpec(shape, lambda i, at: (0, 0)),
            scratch_shapes=[pltpu.SemaphoreType.DMA((len(plan),))],
        ),
        out_shape=jax.ShapeDtypeStruct(shape, LOW),
        compiler_params=pltpu.CompilerParams(vmem_limit_bytes=40 * 2**20),
        cost_estimate=pl.CostEstimate(flops=0, bytes_accessed=4 * shape[0] * shape[1], transcendentals=0),
        name="assemble",
    )(at, *arrays)


def place_over_data(copies, axis=0, shift=0):
    me = lax.axis_index("dp")
    pieces = []
    for mask, val in copies.items():
        at = [shift, shift]
        at[axis] = (me ^ mask) * val.shape[axis]
        pieces.append((val, 0, val.shape[0], at[0], at[1]))
    return pieces


def blocks_over_data(val, axis):
    size = lax.axis_size("dp")
    part = val.shape[axis] // size
    return [
        lax.dynamic_slice_in_dim(val, (lax.axis_index("dp") ^ m) * part, part, axis) for m in range(size)
    ]


def scatter_over_data(blocks):
    order = data_bits(len(blocks))[::-1]
    blocks = dict(enumerate(blocks))
    for bit in order[:-1]:
        out = {}
        for m in [m for m in blocks if not m & bit]:
            out[m] = (blocks[m].astype(FULL) + swap(blocks[m ^ bit], "dp", bit).astype(FULL)).astype(LOW)
        blocks = out
    return blocks[0], blocks[order[-1]]


def last_over_data(sent):
    return swap(sent, "dp", data_bits(lax.axis_size("dp"))[0])


def gain_step(val, bit):
    me = lax.axis_index("dp") * lax.axis_size("seq") + lax.axis_index("seq")
    got = swap_all(val, bit)
    upper = (me // bit) % 2 == 1
    return jnp.concatenate([jnp.where(upper, got, val), jnp.where(upper, val, got)], axis=0)


def output_grad_steps(part, row_ring):
    data, seq = lax.axis_size("dp"), lax.axis_size("seq")
    me = lax.axis_index("dp")
    tall = data // 2
    width = part.shape[1]
    rows = part.shape[0] // (data * seq)
    part = part.reshape(tall, 2, seq, rows, width)
    kept = lax.dynamic_index_in_dim(part, me % 2, 1, False)
    sent = lax.dynamic_index_in_dim(part, 1 - me % 2, 1, False)
    kept = (kept.astype(FULL) + swap(sent, "dp", 1).astype(FULL)).astype(LOW)

    def block(offset):
        one = lax.dynamic_index_in_dim(kept, row_ring.owner(offset), 1, False)
        return one.reshape(tall * rows, width).astype(FULL)

    return row_ring.scatter_steps(block, lambda val: val)


def finish_output_grad(val):
    data = lax.axis_size("dp")
    me = lax.axis_index("dp")
    val = val.reshape(data // 2, -1, val.shape[1])
    _, rows, width = val.shape
    for bit in data_bits(data)[:-1][::-1]:
        upper = (me // bit) % 2
        val = val.reshape(2, val.shape[0] // 2, rows, width)
        kept = lax.dynamic_index_in_dim(val, upper, 0, False)
        sent = lax.dynamic_index_in_dim(val, 1 - upper, 0, False)
        val = kept + swap(sent, "dp", bit)
    return val.reshape(rows, width)


def rms_scale(vals):
    return lax.rsqrt(jnp.mean(vals * vals, axis=-1, keepdims=True) + EPSILON)


def norm_back(grad_out, pre, scale, gain):
    weighted = grad_out * gain
    inner = jnp.mean(weighted * pre, axis=-1, keepdims=True)
    grad_pre = scale * weighted - pre * (scale * scale * scale) * inner
    grad_gain = jnp.sum(grad_out * pre * scale, axis=0)
    return (grad_pre, grad_gain)


def rope_tables(positions):
    half = HEAD // 2
    freq = ROPE_BASE ** (-2.0 * jnp.arange(half, dtype=FULL) / HEAD)
    angle = positions.astype(FULL)[:, None] * freq[None, :]
    cosine, sine = jnp.cos(angle), jnp.sin(angle)
    return jnp.concatenate([cosine, cosine], 1), jnp.concatenate([-sine, sine], 1)


def layout(lengths, placement, row_len):
    stored, docs = lengths.shape
    rows = jnp.arange(placement.shape[0], dtype=jnp.int32)
    row = jnp.sum(jnp.where(rows == lax.axis_index("dp"), placement, 0))
    doc_lens = jnp.sum(
        jnp.where(jnp.arange(stored, dtype=jnp.int32)[:, None] == row, lengths, 0), axis=0
    )
    upto = jnp.arange(docs, dtype=jnp.int32)
    doc_ends = jnp.sum(jnp.where(upto[None, :] <= upto[:, None], doc_lens[None, :], 0), axis=1)
    at = jnp.arange(row_len, dtype=jnp.int32)
    passed = at[:, None] >= doc_ends[None, :]
    return jnp.max(jnp.where(passed, doc_ends[None, :], 0), axis=1)


def column(row):
    return jnp.broadcast_to(row, (HEAD, row.shape[1])).T

def attend_forward_kernel(first_ref, q_ref, k_ref, v_ref, scale_ref, gain_ref, cos_ref, sin_ref, begin_ref,
                          out_ref, qr_ref, kr_ref, vl_ref, lse_ref, vt_ref):
    blocks = q_ref.shape[0] // BLOCK
    factor = HEAD ** -0.5 * LOG2E

    def prepare(i, _):
        rows = pl.ds(pl.multiple_of(i * BLOCK, BLOCK), BLOCK)
        for n, (src, dst) in enumerate(((q_ref, qr_ref), (k_ref, kr_ref))):
            x = src[rows, :] * column(scale_ref[n : n + 1, rows]) * gain_ref[n : n + 1, :]
            x = x * cos_ref[rows, :] + pltpu.roll(x, HEAD // 2, 1) * sin_ref[rows, :]
            dst[rows, :] = x.astype(LOW)
        v = v_ref[rows, :].astype(LOW)
        vl_ref[rows, :] = v
        vt_ref[:, rows] = v.T
        return 0

    lax.fori_loop(0, blocks, prepare, 0)

    def one(i, _):
        rows = pl.ds(pl.multiple_of(i * BLOCK, BLOCK), BLOCK)
        q = qr_ref[rows, :]
        begin = begin_ref[0:1, rows]
        at = lax.broadcasted_iota(jnp.int32, (BLOCK, BLOCK), 0)
        query_at = lax.broadcasted_iota(jnp.int32, (1, BLOCK), 1) + i * BLOCK

        def step(j, carry):
            top, total, acc = carry
            keys = pl.ds(pl.multiple_of(j * BLOCK, BLOCK), BLOCK)
            s = dot_nt(kr_ref[keys, :], q)
            key_at = at + j * BLOCK
            s = jnp.where((key_at >= begin) & (key_at <= query_at), s, NEG)
            new = jnp.maximum(top, jnp.max(s, axis=0, keepdims=True))
            p = jnp.exp2((s - new) * factor)
            shrink = jnp.exp2((top - new) * factor)
            total = total * shrink + jnp.sum(p, axis=0, keepdims=True)
            acc = acc * shrink + dot(vt_ref[:, keys], p.astype(LOW))
            return new, total, acc

        start = (jnp.full((1, BLOCK), NEG, FULL), jnp.zeros((1, BLOCK), FULL), jnp.zeros((HEAD, BLOCK), FULL))
        top, total, acc = lax.fori_loop(first_ref[i], i + 1, step, start)
        out_ref[rows, :] = (acc / total).T.astype(LOW)
        lse_ref[0, 0:1, rows] = top * factor + jnp.log2(total)
        return 0

    lax.fori_loop(0, blocks, one, 0)


def attend_forward(pre, scales, gains, cosine, sine, first, begin):
    rows, wide = pre.shape
    heads = wide // (3 * HEAD)

    def col(shift):
        return pl.BlockSpec((rows, HEAD), lambda h, f: (0, h + shift))

    def fixed(*shape):
        return pl.BlockSpec(shape, lambda h, f: (0,) * len(shape))

    return pl.pallas_call(
        attend_forward_kernel,
        grid_spec=pltpu.PrefetchScalarGridSpec(
            num_scalar_prefetch=1,
            grid=(heads,),
            in_specs=[
                col(0),
                col(heads),
                col(2 * heads),
                fixed(2, rows),
                pl.BlockSpec((2, HEAD), lambda h, f: (0, h)),
                fixed(rows, HEAD),
                fixed(rows, HEAD),
                fixed(1, rows),
            ],
            out_specs=[col(0)] * 4 + [pl.BlockSpec((1, 1, rows), lambda h, f: (h, 0, 0))],
            scratch_shapes=[pltpu.VMEM((HEAD, rows), LOW)],
        ),
        out_shape=[jax.ShapeDtypeStruct((rows, heads * HEAD), LOW)] * 4
        + [jax.ShapeDtypeStruct((heads, 1, rows), FULL)],
        compiler_params=pltpu.CompilerParams(vmem_limit_bytes=48 * 2**20),
        cost_estimate=LIGHT,
        name="attend_forward",
    )(first, pre, pre, pre, scales, gains, cosine, sine, begin)


def attend_backward_kernel(first_ref, q_ref, k_ref, v_ref, o_ref, do_ref, lse_ref, qp_ref, kp_ref, scale_ref, gain_ref, cos_ref, sin_ref, begin_ref,
                           gq_ref, gk_ref, gv_ref, inner_ref, gain_grad_ref, kt_ref, dk_ref, dv_ref):
    blocks = q_ref.shape[0] // BLOCK
    norm = HEAD ** -0.5
    factor = norm * LOG2E

    def prepare(i, _):
        rows = pl.ds(pl.multiple_of(i * BLOCK, BLOCK), BLOCK)
        kt_ref[:, rows] = k_ref[rows, :].T
        dk_ref[rows, :] = jnp.zeros((BLOCK, HEAD), FULL)
        dv_ref[rows, :] = jnp.zeros((BLOCK, HEAD), FULL)
        return 0

    lax.fori_loop(0, blocks, prepare, 0)

    def finish(rows, n, grad, pre_ref, out):
        grad = grad.astype(LOW).astype(FULL)
        grad = grad * cos_ref[rows, :] - pltpu.roll(grad, HEAD // 2, 1) * sin_ref[rows, :]
        weighted = grad * gain_ref[n : n + 1, :]
        pre = pre_ref[rows, :]
        out[rows, :] = weighted
        inner_ref[0, n : n + 1, rows] = jnp.sum((weighted * pre).T, axis=0, keepdims=True)
        return jnp.sum(grad * pre * column(scale_ref[n : n + 1, rows]), axis=0, keepdims=True)

    def one(i, gain_grad):
        rows = pl.ds(pl.multiple_of(i * BLOCK, BLOCK), BLOCK)
        q = q_ref[rows, :]
        do = do_ref[rows, :]
        begin = begin_ref[0:1, rows]
        lse = lse_ref[0, 0:1, rows]
        delta = jnp.sum((do.astype(FULL) * o_ref[rows, :].astype(FULL)).T, axis=0, keepdims=True)
        at = lax.broadcasted_iota(jnp.int32, (BLOCK, BLOCK), 0)
        query_at = lax.broadcasted_iota(jnp.int32, (1, BLOCK), 1) + i * BLOCK

        def step(j, acc):
            keys = pl.ds(pl.multiple_of(j * BLOCK, BLOCK), BLOCK)
            s = dot_nt(k_ref[keys, :], q)
            key_at = at + j * BLOCK
            s = jnp.where((key_at >= begin) & (key_at <= query_at), s, NEG)
            p = jnp.exp2(s * factor - lse)
            dp = dot_nt(v_ref[keys, :], do)
            ds = (p * (dp - delta)).astype(LOW)
            dv_ref[keys, :] += dot(p.astype(LOW), do)
            dk_ref[keys, :] += dot(ds, q)
            return acc + dot(kt_ref[:, keys], ds)

        acc = lax.fori_loop(first_ref[i], i + 1, step, jnp.zeros((HEAD, BLOCK), FULL))
        return gain_grad + finish(rows, 0, acc.T * norm, qp_ref, gq_ref)

    gain_grad_ref[0:1, :] = lax.fori_loop(0, blocks, one, jnp.zeros((1, HEAD), FULL))

    def close(i, gain_grad):
        rows = pl.ds(pl.multiple_of(i * BLOCK, BLOCK), BLOCK)
        gv_ref[rows, :] = dv_ref[rows, :].astype(LOW)
        return gain_grad + finish(rows, 1, dk_ref[rows, :] * norm, kp_ref, gk_ref)

    gain_grad_ref[1:2, :] = lax.fori_loop(0, blocks, close, jnp.zeros((1, HEAD), FULL))


def attend_backward(head, q, k, v, out, grad, lse, pre, scales, gains, cosine, sine, first, begin):
    rows = q.shape[0]
    heads = pre.shape[1] // (3 * HEAD)

    def col(shift):
        return pl.BlockSpec((rows, HEAD), lambda i, f: (0, shift))

    def fixed(*shape):
        return pl.BlockSpec(shape, lambda i, f: (0,) * len(shape))

    full = jax.ShapeDtypeStruct((rows, HEAD), FULL)
    return pl.pallas_call(
        attend_backward_kernel,
        grid_spec=pltpu.PrefetchScalarGridSpec(
            num_scalar_prefetch=1,
            grid=(1,),
            in_specs=[col(head)] * 5
            + [
                pl.BlockSpec((1, 1, rows), lambda i, f: (head, 0, 0)),
                col(head),
                col(heads + head),
                fixed(2, rows),
                pl.BlockSpec((2, HEAD), lambda i, f: (0, head)),
                fixed(rows, HEAD),
                fixed(rows, HEAD),
                fixed(1, rows),
            ],
            out_specs=[fixed(rows, HEAD)] * 3 + [fixed(1, 2, rows), fixed(2, HEAD)],
            scratch_shapes=[
                pltpu.VMEM((HEAD, rows), LOW),
                pltpu.VMEM((rows, HEAD), FULL),
                pltpu.VMEM((rows, HEAD), FULL),
            ],
        ),
        out_shape=[
            full,
            full,
            jax.ShapeDtypeStruct((rows, HEAD), LOW),
            jax.ShapeDtypeStruct((1, 2, rows), FULL),
            jax.ShapeDtypeStruct((2, HEAD), FULL),
        ],
        compiler_params=pltpu.CompilerParams(vmem_limit_bytes=48 * 2**20),
        cost_estimate=LIGHT,
        name="attend_backward",
    )(first, q, k, v, out, grad, lse, pre, pre, scales, gains, cosine, sine, begin)


def per_device(
    tokens,
    cotangent,
    lengths,
    placement,
    w_query,
    w_key,
    w_value,
    w_output,
    query_gain,
    key_gain,
    attn_gain,
    w_gate,
    w_up,
    w_down,
    mlp_gain,
):
    data, seq = lax.axis_size("dp"), lax.axis_size("seq")
    seq_at = lax.axis_index("seq")
    _, count, width = tokens.shape
    row_len = count * seq
    own = width // seq
    row_ring = Ring([row_cycle(seq)])
    inputs = tokens.reshape(count, width)
    begin = layout(lengths, placement, row_len)

    packed = jnp.stack([w_query, w_key, w_value], axis=1).reshape(-1, 3, seq, own)
    packed = jnp.moveaxis(packed, 2, 0).reshape(seq, -1, 3 * own)
    hid = w_gate.shape[1]
    chips = data_bits(data)[:-1]
    state = {"gains": jnp.stack([query_gain, key_gain, attn_gain, mlp_gain])[None]}
    gain_bits = [b * seq for b in data_bits(data)] + bits_of(seq)
    gain_order = list(gain_bits)

    def more_gains():
        if gain_bits:
            state["gains"] = gain_step(state["gains"], gain_bits.pop(0))

    def beside(step, chunks):
        more_gains()
        if step == 1:
            state["down"] = swap_chips(w_down, chips)
            state["w_heads"] = lax.all_to_all(packed, "seq", split_axis=0, concat_axis=0, tiled=True)
            return ["gains"]
        if step == 2:
            state["gate"] = swap_chips(w_gate, chips)
            return ["gains", "w_heads", "down", "gate", "begin"]
        if step == 3:
            state["w_heads"] = swap_chips(state["w_heads"].reshape(-1, 3 * own), chips)
            state["up"] = w_up
            return ["gains", "w_heads", "up"]
        return ["gains"]

    state["begin"] = begin
    row_chunks = row_ring.gather(inputs, state, beside)
    begin = state["begin"]
    first_block = begin[::BLOCK] // BLOCK
    cosine, sine = rope_tables(jnp.arange(row_len, dtype=jnp.int32) - begin)
    begin = begin[None]
    state["up"] = swap_chips(state["up"], chips)
    last = row_ring.size // 2
    row_tokens = jnp.zeros((row_len, width), LOW)
    for offset, chunk in row_chunks.items():
        if offset == last:
            chunk, w_out, row_tokens, cosine, sine = tie(
                chunk, w_output, row_tokens, cosine, sine
            )
        row_tokens = lax.dynamic_update_slice(row_tokens, chunk, (row_ring.owner(offset) * count, 0))
    w_out = lax.all_gather(w_out, ("dp", "seq"), axis=0, tiled=True)
    w_heads = assemble((width, 3 * own), place_over_data(swap_cores(state["w_heads"])))
    pre = dot(row_tokens, w_heads)
    while gain_bits:
        more_gains()
    placed = [gain_order[::-1].index(bit) for bit in sorted(gain_order, reverse=True)]
    gains = state["gains"].reshape((2,) * len(placed) + state["gains"].shape[1:])
    gains = jnp.transpose(gains, [len(placed)] + placed + [len(placed) + 1])
    gains = gains.reshape(4, -1).astype(FULL)
    gain_attn, gain_mlp = gains[2], gains[3]
    gains_own = lax.dynamic_slice(gains, (0, seq_at * own), (2, own))
    query_pre, key_pre = pre[:, :own], pre[:, own : 2 * own]
    squares = jnp.stack([jnp.sum(query_pre * query_pre, axis=1), jnp.sum(key_pre * key_pre, axis=1)])
    scales = lax.rsqrt(sum_over(squares, "seq", seq) / width + EPSILON)
    scales, state["up"] = tie(scales, state["up"])
    attn_heads, query_rot, key_rot, values, log_sums = attend_forward(
        pre, scales, gains_own, cosine, sine, first_block, begin
    )
    attn_tokens = lax.all_to_all(
        attn_heads.reshape(seq, count, own), "seq", split_axis=0, concat_axis=0, tiled=True
    )
    attn_tokens = jnp.moveaxis(attn_tokens, 0, 1).reshape(count, width)

    attn_pre = dot(attn_tokens, w_out)
    attn_scale = rms_scale(attn_pre)
    middle = inputs.astype(FULL) + attn_pre * attn_scale * gain_attn
    middle_low = middle.astype(LOW)

    mids = row_ring.gather(middle_low)
    near, mids[0] = tie([state[n] for n in ("gate", "up", "down")], mids[0])
    near = [swap_cores(n) for n in near]
    gate_up = assemble((width, 2 * hid), place_over_data(near[0]) + place_over_data(near[1], 0, hid))
    down = assemble((hid, width), place_over_data(near[2], 1))
    saved = {}

    def mlp_part(offset):
        offset = offset if offset in mids else -offset
        both = dot(mids[offset], gate_up)
        gate, up = both[:, :hid], both[:, hid:]
        hidden = (gate * jax.nn.sigmoid(gate) * up).astype(LOW)
        saved[offset] = gate, up, hidden
        return dot(hidden, down)

    mlp_pre = row_ring.scatter(mlp_part)
    mlp_scale = rms_scale(mlp_pre)
    layer_out = (middle + mlp_pre * mlp_scale * gain_mlp).astype(LOW).reshape(tokens.shape)
    grad_final = cotangent.reshape(count, width).astype(FULL)
    grad_mlp_pre, grad_gain_mlp = norm_back(grad_final, mlp_pre, mlp_scale, gain_mlp)
    grads = row_ring.gather(grad_mlp_pre.astype(LOW))
    grad_both = {}

    def middle_part(offset):
        gate, up, hidden = saved[offset]
        grad_hidden = dot_nt(grads[offset], down)
        sig = jax.nn.sigmoid(gate)
        grad_gate = grad_hidden * up * sig * (1.0 + gate * (1.0 - sig))
        grad_up = grad_hidden * gate * sig
        grad_both[offset] = grad_gate.astype(LOW), grad_up.astype(LOW)
        return dot_nt(jnp.concatenate(grad_both[offset], axis=1), gate_up)

    order = list(mids)
    ffn = {"mids": jnp.concatenate([mids[o] for o in order])}
    ffn["grads"] = jnp.concatenate([grads[o] for o in order])
    ffn["hidden"] = jnp.concatenate([saved[o][2] for o in order])

    half = row_ring.size // 2

    def beside_middle(step, sent):
        if step == half - 2:
            ffn["down"] = dot_tn(ffn["hidden"], ffn["grads"]).astype(LOW)
            sent, ffn["down"] = tie(sent, ffn["down"])
        if step == half - 1:
            rows = jnp.concatenate([grad_both[o][0] for o in order])
            ffn["gate"] = dot_tn(ffn["mids"], rows).astype(LOW)
            sent, ffn["gate"], ffn["down"] = tie(sent, ffn["gate"], ffn["down"])
        return sent

    middle_parts = {o: middle_part(o) for o in order}
    grad_middle = row_ring.scatter(lambda o: middle_parts[o], beside_middle)
    rows = jnp.concatenate([grad_both[o][1] for o in order])
    ffn["up"] = dot_tn(ffn["mids"], rows).astype(LOW)
    sums = {n: scatter_over_data(blocks_over_data(ffn[n], a)) for n, a in (("down", 1), ("gate", 0))}
    grad_middle, sums, ffn["up"] = tie(grad_middle, sums, ffn["up"])
    grad_middle = grad_final + grad_middle

    grad_attn_pre, grad_gain_attn = norm_back(grad_middle, attn_pre, attn_scale, gain_attn)
    grad_attn_low = grad_attn_pre.astype(LOW)
    grad_heads = dot_nt(grad_attn_low, w_out).astype(LOW)
    grad_heads, grad_attn_low = tie(grad_heads, grad_attn_low)
    grad_heads = jnp.moveaxis(grad_heads.reshape(count, seq, own), 1, 0)
    grad_heads = lax.all_to_all(grad_heads, "seq", split_axis=0, concat_axis=0, tiled=True)
    grad_heads = grad_heads.reshape(row_len, own)
    steps = output_grad_steps(dot_tn(attn_tokens, grad_attn_low).astype(LOW), row_ring)
    sent = next(steps)
    sums["up"] = scatter_over_data(blocks_over_data(ffn["up"], 0))
    got = {n: last_over_data(sums[n][1]) for n in ("down", "gate")}
    grad_heads, sent, sums["up"] = tie(grad_heads, sent, sums["up"])
    got["up"] = last_over_data(sums["up"][1])
    sums = {n: val[0] for n, val in sums.items()}
    heads = []
    for head in range(own // HEAD):
        if head:
            sent = steps.send(sent)
            grad_heads, sent, *early = tie(grad_heads, sent, got["down"], got["gate"])
            got["down"], got["gate"] = early
        done = attend_backward(
            head,
            query_rot,
            key_rot,
            values,
            attn_heads,
            grad_heads,
            log_sums,
            pre,
            scales,
            gains_own,
            cosine,
            sine,
            first_block,
            begin,
        )
        heads.append(list(done))
    sent = steps.send(sent)
    weighted_q, weighted_k, grad_v = (
        jnp.concatenate([h[i] for h in heads], axis=1) for i in range(3)
    )
    inner = sum(h[3][0] for h in heads)
    inner, sent, got["up"] = tie(inner, sent, got["up"])
    gain_part = jnp.concatenate([h[4] for h in heads], axis=1)
    gain_part = lax.dynamic_update_slice(jnp.zeros((2, width), FULL), gain_part, (0, seq_at * own))
    inner = jnp.concatenate([inner, jnp.zeros((2, width - row_len), FULL)], axis=1)
    small = jnp.concatenate([inner, gain_part, grad_gain_attn[None], grad_gain_mlp[None]])
    small = sum_over(small, "seq", seq)
    inner, gain_sums = small[:2, :row_len], small[2:]
    last_sent = steps.send(sent)
    inner = inner * (scales**3) / width
    by_token = jnp.concatenate([scales, inner]).T
    grad_qp = by_token[:, 0:1] * weighted_q - by_token[:, 2:3] * query_pre
    grad_kp = by_token[:, 1:2] * weighted_k - by_token[:, 3:4] * key_pre
    grad_pre = jnp.concatenate([grad_qp.astype(LOW), grad_kp.astype(LOW), grad_v], axis=1)

    rest = {"pre": grad_pre, "output": last_sent, "sums": sums, "got": got}

    token_parts = dot_nt(grad_pre, w_heads).astype(LOW)

    def token_part(offset):
        start = row_ring.owner(offset) * count
        return lax.dynamic_slice_in_dim(token_parts, start, count, 0).astype(FULL)

    def beside_tokens(step, sent):
        names = ["pre"]
        if step == 1:
            names += ["sums", "got", "output"]
        if step == 2:
            rest["part"] = dot_tn(row_tokens, rest["pre"]).astype(LOW)
            names += ["part"]
        if step == 3:
            rest["part"] = scatter_over_data(blocks_over_data(rest["part"], 0))
            rest["part"] = rest["part"][0], last_over_data(rest["part"][1])
            names += ["part"]
        sent, *tied = tie(sent, *(rest[n] for n in names))
        rest.update(zip(names, tied))
        return sent

    grad_tokens = grad_middle + finish(
        row_ring.scatter_steps(token_part, lambda val: val), beside_tokens
    )
    grad_tokens = grad_tokens.astype(LOW).reshape(tokens.shape)
    gain_sums = sum_over(gain_sums, "dp", data)
    share = width // (data * seq)
    start = (lax.axis_index("dp") * seq + seq_at) * share
    gain_grads = lax.dynamic_slice(gain_sums, (0, start), (4, share))
    part = (rest["part"][0].astype(FULL) + rest["part"][1].astype(FULL)).astype(LOW)
    part = lax.all_to_all(
        part.reshape(seq, -1, 3 * own), "seq", split_axis=0, concat_axis=0, tiled=True
    )
    grad_query, grad_key, grad_value = (
        jnp.concatenate([part[d, :, n * own : (n + 1) * own] for d in range(seq)], axis=1).astype(FULL)
        for n in range(3)
    )
    sums, got = rest["sums"], rest["got"]
    grad_output = finish_output_grad(finish(steps, sent=rest["output"]))
    grad_down, grad_gate, grad_up = (
        sums[n].astype(FULL) + got[n].astype(FULL) for n in ("down", "gate", "up")
    )

    return (
        layer_out,
        grad_tokens,
        grad_query,
        grad_key,
        grad_value,
        grad_output,
        gain_grads[0],
        gain_grads[1],
        gain_grads[2],
        grad_gate,
        grad_up,
        grad_down,
        gain_grads[3],
    )


def solution(mesh):
    rows = P("dp", "seq", None)
    both = P(("dp", "seq"), None)
    flat = P(("dp", "seq"))
    return jax.shard_map(
        per_device,
        mesh=mesh,
        in_specs=(rows, rows, P(), P())
        + (both,) * 4
        + (flat,) * 3
        + (P("dp", "seq"), P("dp", "seq"), P("seq", "dp"), flat),
        out_specs=(rows, rows)
        + (both,) * 4
        + (flat,) * 3
        + (P("dp", "seq"), P("dp", "seq"), P("seq", "dp"), flat),
        check_vma=False,
    )
```

```python
import math

import jax
import jax.numpy as jnp
from jax import lax
from jax.experimental import pallas as pl
from jax.experimental.pallas import tpu as pltpu
from jax.sharding import PartitionSpec as P

HEAD = 128
LEVELS = 4
EPSILON = 1e-06
ROPE_BASE = 500000.0
LOW = jnp.bfloat16
FULL = jnp.float32
NEG = -1e30
LOG2E = math.log2(math.e)
LIGHT = pl.CostEstimate(flops=1, bytes_accessed=1, transcendentals=0)
BLOCK = 512


def dot(left, right):
    return jnp.dot(left, right, preferred_element_type=FULL)


def dot_nt(left, right):
    return lax.dot_general(left, right, (((1,), (1,)), ((), ())), preferred_element_type=FULL)


def dot_tn(left, right):
    return lax.dot_general(left, right, (((0,), (0,)), ((), ())), preferred_element_type=FULL)


def swap(val, axis, mask):
    size = lax.axis_size(axis)
    return lax.ppermute(val, axis, [(i, i ^ mask) for i in range(size)])


def swap_all(val, mask):
    size = lax.axis_size("dp") * lax.axis_size("seq")
    return lax.ppermute(val, ("dp", "seq"), [(i, i ^ mask) for i in range(size)])


def tie(*vals):
    return lax.optimization_barrier(vals)


def bits_of(size):
    return [1 << i for i in range(size.bit_length() - 1)]


def sum_over(val, axis, size):
    for bit in bits_of(size):
        val = val + swap(val, axis, bit)
    return val


class Ring:
    def __init__(self, cycles):
        self.size = len(cycles[0])
        self.forth = [(c[i], c[(i + 1) % self.size]) for c in cycles for i in range(self.size)]
        self.back = [(b, a) for a, b in self.forth]
        total = self.size * len(cycles)
        owners = [[0] * self.size for _ in range(total)]
        for c in cycles:
            for i, dev in enumerate(c):
                for off in range(self.size):
                    owners[dev][off] = c[(i + off) % self.size]
        self.owners = owners

    def owner(self, offset):
        at = lax.axis_index("seq")
        found = jnp.int32(self.owners[0][offset % self.size])
        for dev, row in enumerate(self.owners[1:], 1):
            found = lax.select(at == dev, jnp.int32(row[offset % self.size]), found)
        return found

    def right(self, val):
        return lax.ppermute(val, "seq", self.forth)

    def left(self, val):
        return lax.ppermute(val, "seq", self.back)

    def gather(self, own, state=None, between=None):
        half = self.size // 2
        chunks = {0: own}
        r = l = own
        for k in range(1, half):
            r, l = self.right(r), self.left(l)
            chunks[-k], chunks[k] = r, l
            names = between(k, chunks) if between else ()
            if names:
                r, l, *beside = tie(r, l, *(state[n] for n in names))
                state |= dict(zip(names, beside))
        mid = own.shape[0] // 2
        chunks[half] = jnp.concatenate([self.right(r[:mid]), self.left(l[mid:])], axis=0)
        return chunks

    def scatter_steps(self, part, hold=lax.optimization_barrier):
        half = self.size // 2
        far = part(half).astype(LOW)
        mid = far.shape[0] // 2
        r, l = yield far[:mid], far[mid:]
        r, l = self.right(r), self.left(l)
        zero = jnp.zeros((), LOW)
        r = lax.pad(r, zero, ((0, mid, 0), (0, 0, 0)))
        l = lax.pad(l, zero, ((mid, 0, 0), (0, 0, 0)))
        for k in range(half - 1, 0, -1):
            a = hold(part(k)) + r.astype(FULL)
            b = hold(part(-k)) + l.astype(FULL)
            r, l = yield a.astype(LOW), b.astype(LOW)
            r, l = self.right(r), self.left(l)
        return hold(part(0)) + r.astype(FULL) + l.astype(FULL)

    def scatter(self, part, hook=None):
        return finish(self.scatter_steps(part), hook)


def finish(steps, hook=None, sent=None, step=0):
    try:
        sent = next(steps) if sent is None else sent
        while True:
            sent = steps.send(hook(step, sent) if hook else sent)
            step += 1
    except StopIteration as end:
        return end.value


def row_cycle(size):
    if size % LEVELS or size == LEVELS:
        return list(range(size))
    cols = size // LEVELS
    walk = [(0, 0)]
    for z in range(LEVELS):
        span = list(range(1, cols))
        walk += [(z, x) for x in (span if z % 2 == 0 else span[::-1])]
    walk += [(z, 0) for z in range(LEVELS - 1, 0, -1)]
    return [z * cols + x for z, x in walk]


def data_bits(size):
    return [b for b in bits_of(size) if b != 1] + [1]


def swap_chips(shard, bits):
    copies = {0: shard}
    for bit in bits:
        copies |= {mask ^ bit: swap(val, "dp", bit) for mask, val in copies.items()}
    return copies


def swap_cores(copies):
    return copies | {mask ^ 1: swap(val, "dp", 1) for mask, val in copies.items()}


def assemble_kernel(plan, at_ref, *refs):
    out_ref, sems = refs[-2], refs[-1]
    copies = []
    for i, (source, row, rows) in enumerate(plan):
        cols = refs[source].shape[1]
        place = (
            pl.ds(pl.multiple_of(at_ref[2 * i], 16), rows),
            pl.ds(pl.multiple_of(at_ref[2 * i + 1], 128), cols),
        )
        copies.append(
            pltpu.make_async_copy(refs[source].at[pl.ds(row, rows), :], out_ref.at[place], sems.at[i])
        )
    for copy in copies:
        copy.start()
    for copy in copies:
        copy.wait()


def assemble(shape, pieces):
    arrays, plan, at = [], [], []
    for val, row, rows, to_row, to_col in pieces:
        known = [i for i, a in enumerate(arrays) if a is val]
        if not known:
            arrays.append(val)
        plan.append((known[0] if known else len(arrays) - 1, row, rows))
        at += [to_row, to_col]
    at = jnp.stack([jnp.asarray(a, jnp.int32) for a in at])
    return pl.pallas_call(
        lambda at_ref, *refs: assemble_kernel(plan, at_ref, *refs),
        grid_spec=pltpu.PrefetchScalarGridSpec(
            num_scalar_prefetch=1,
            grid=(1,),
            in_specs=[pl.BlockSpec(memory_space=pl.ANY)] * len(arrays),
            out_specs=pl.BlockSpec(shape, lambda i, at: (0, 0)),
            scratch_shapes=[pltpu.SemaphoreType.DMA((len(plan),))],
        ),
        out_shape=jax.ShapeDtypeStruct(shape, LOW),
        compiler_params=pltpu.CompilerParams(vmem_limit_bytes=40 * 2**20),
        cost_estimate=pl.CostEstimate(flops=0, bytes_accessed=4 * shape[0] * shape[1], transcendentals=0),
        name="assemble",
    )(at, *arrays)


def place_over_data(copies, axis=0, shift=0):
    me = lax.axis_index("dp")
    pieces = []
    for mask, val in copies.items():
        at = [shift, shift]
        at[axis] = (me ^ mask) * val.shape[axis]
        pieces.append((val, 0, val.shape[0], at[0], at[1]))
    return pieces


def blocks_over_data(val, axis):
    size = lax.axis_size("dp")
    part = val.shape[axis] // size
    return [
        lax.dynamic_slice_in_dim(val, (lax.axis_index("dp") ^ m) * part, part, axis) for m in range(size)
    ]


def scatter_over_data(blocks):
    order = data_bits(len(blocks))[::-1]
    blocks = dict(enumerate(blocks))
    for bit in order[:-1]:
        out = {}
        for m in [m for m in blocks if not m & bit]:
            out[m] = (blocks[m].astype(FULL) + swap(blocks[m ^ bit], "dp", bit).astype(FULL)).astype(LOW)
        blocks = out
    return blocks[0], blocks[order[-1]]


def last_over_data(sent):
    return swap(sent, "dp", data_bits(lax.axis_size("dp"))[0])


def gain_step(val, bit):
    me = lax.axis_index("dp") * lax.axis_size("seq") + lax.axis_index("seq")
    got = swap_all(val, bit)
    upper = (me // bit) % 2 == 1
    return jnp.concatenate([jnp.where(upper, got, val), jnp.where(upper, val, got)], axis=0)


def output_grad_steps(part, row_ring):
    data, seq = lax.axis_size("dp"), lax.axis_size("seq")
    me = lax.axis_index("dp")
    tall = data // 2
    width = part.shape[1]
    rows = part.shape[0] // (data * seq)
    part = part.reshape(tall, 2, seq, rows, width)
    kept = lax.dynamic_index_in_dim(part, me % 2, 1, False)
    sent = lax.dynamic_index_in_dim(part, 1 - me % 2, 1, False)
    kept = (kept.astype(FULL) + swap(sent, "dp", 1).astype(FULL)).astype(LOW)

    def block(offset):
        one = lax.dynamic_index_in_dim(kept, row_ring.owner(offset), 1, False)
        return one.reshape(tall * rows, width).astype(FULL)

    return row_ring.scatter_steps(block, lambda val: val)


def finish_output_grad(val):
    data = lax.axis_size("dp")
    me = lax.axis_index("dp")
    val = val.reshape(data // 2, -1, val.shape[1])
    _, rows, width = val.shape
    for bit in data_bits(data)[:-1][::-1]:
        upper = (me // bit) % 2
        val = val.reshape(2, val.shape[0] // 2, rows, width)
        kept = lax.dynamic_index_in_dim(val, upper, 0, False)
        sent = lax.dynamic_index_in_dim(val, 1 - upper, 0, False)
        val = kept + swap(sent, "dp", bit)
    return val.reshape(rows, width)


def rms_scale(vals):
    return lax.rsqrt(jnp.mean(vals * vals, axis=-1, keepdims=True) + EPSILON)


def norm_back(grad_out, pre, scale, gain):
    weighted = grad_out * gain
    inner = jnp.mean(weighted * pre, axis=-1, keepdims=True)
    grad_pre = scale * weighted - pre * (scale * scale * scale) * inner
    grad_gain = jnp.sum(grad_out * pre * scale, axis=0)
    return (grad_pre, grad_gain)


def rope_tables(positions):
    half = HEAD // 2
    freq = ROPE_BASE ** (-2.0 * jnp.arange(half, dtype=FULL) / HEAD)
    angle = positions.astype(FULL)[:, None] * freq[None, :]
    cosine, sine = jnp.cos(angle), jnp.sin(angle)
    return jnp.concatenate([cosine, cosine], 1), jnp.concatenate([-sine, sine], 1)


def layout(lengths, placement, row_len):
    stored, docs = lengths.shape
    rows = jnp.arange(placement.shape[0], dtype=jnp.int32)
    row = jnp.sum(jnp.where(rows == lax.axis_index("dp"), placement, 0))
    doc_lens = jnp.sum(
        jnp.where(jnp.arange(stored, dtype=jnp.int32)[:, None] == row, lengths, 0), axis=0
    )
    upto = jnp.arange(docs, dtype=jnp.int32)
    doc_ends = jnp.sum(jnp.where(upto[None, :] <= upto[:, None], doc_lens[None, :], 0), axis=1)
    at = jnp.arange(row_len, dtype=jnp.int32)
    passed = at[:, None] >= doc_ends[None, :]
    return jnp.max(jnp.where(passed, doc_ends[None, :], 0), axis=1)


def column(row):
    return jnp.broadcast_to(row, (HEAD, row.shape[1])).T

def attend_forward_kernel(
    first_ref,
    q_ref,
    k_ref,
    v_ref,
    scale_ref,
    gain_ref,
    cos_ref,
    sin_ref,
    begin_ref,
    out_ref,
    qr_ref,
    kr_ref,
    vl_ref,
    lse_ref,
    keys_ref,
    vt_ref,
):
    i = pl.program_id(0)
    rows = pl.ds(pl.multiple_of(i * BLOCK, BLOCK), BLOCK)
    heads = [slice(at, at + HEAD) for at in range(0, q_ref.shape[1], HEAD)]
    factor = HEAD**-0.5 * LOG2E
    for n, (src, dst) in enumerate(((q_ref, qr_ref), (k_ref, kr_ref))):
        scale = column(scale_ref[n : n + 1, :])
        for head in heads:
            x = src[:, head] * scale * gain_ref[n : n + 1, head]
            x = x * cos_ref[...] + pltpu.roll(x, HEAD // 2, 1) * sin_ref[...]
            dst[:, head] = x.astype(LOW)
    keys_ref[rows, :] = kr_ref[...]
    for head in heads:
        v = v_ref[:, head].astype(LOW)
        vl_ref[:, head] = v
        vt_ref[head, rows] = v.T
    begin = begin_ref[0:1, :]
    at = lax.broadcasted_iota(jnp.int32, (BLOCK, BLOCK), 0)
    query_at = lax.broadcasted_iota(jnp.int32, (1, BLOCK), 1) + i * BLOCK

    def step(j, carry):
        keys = pl.ds(pl.multiple_of(j * BLOCK, BLOCK), BLOCK)
        key_at = at + j * BLOCK
        keep = (key_at >= begin) & (key_at <= query_at)
        scores = [
            jnp.where(keep, dot_nt(keys_ref[keys, head], qr_ref[:, head]), NEG) for head in heads
        ]
        out = []
        for head, s, (top, total, acc) in zip(heads, scores, carry):
            new = jnp.maximum(top, jnp.max(s, axis=0, keepdims=True))
            p = jnp.exp2((s - new) * factor)
            shrink = jnp.exp2((top - new) * factor)
            total = total * shrink + jnp.sum(p, axis=0, keepdims=True)
            acc = acc * shrink + dot(vt_ref[head, keys], p.astype(LOW))
            out.append((new, total, acc))
        return tuple(out)

    start = (
        jnp.full((1, BLOCK), NEG, FULL),
        jnp.zeros((1, BLOCK), FULL),
        jnp.zeros((HEAD, BLOCK), FULL),
    )
    done = lax.fori_loop(first_ref[i], i + 1, step, (start,) * len(heads))
    for h, (top, total, acc) in enumerate(done):
        out_ref[:, heads[h]] = (acc / total).T.astype(LOW)
        lse_ref[h, 0:1, :] = top * factor + jnp.log2(total)


def attend_forward(pre, scales, gains, cosine, sine, first, begin):
    rows, wide = pre.shape
    own = wide // 3

    def part(cols, at=0):
        return pl.BlockSpec((BLOCK, cols), lambda i, f: (i, at))

    def along(*lead):
        return pl.BlockSpec((*lead, BLOCK), lambda i, f: (0,) * len(lead) + (i,))

    return pl.pallas_call(
        attend_forward_kernel,
        grid_spec=pltpu.PrefetchScalarGridSpec(
            num_scalar_prefetch=1,
            grid=(rows // BLOCK,),
            in_specs=[part(own), part(own, 1), part(own, 2), along(2)]
            + [pl.BlockSpec((2, own), lambda i, f: (0, 0)), part(HEAD), part(HEAD), along(1)],
            out_specs=[part(own)] * 4 + [along(own // HEAD, 1)],
            scratch_shapes=[pltpu.VMEM((rows, own), LOW), pltpu.VMEM((own, rows), LOW)],
        ),
        out_shape=[jax.ShapeDtypeStruct((rows, own), LOW)] * 4
        + [jax.ShapeDtypeStruct((own // HEAD, 1, rows), FULL)],
        compiler_params=pltpu.CompilerParams(vmem_limit_bytes=48 * 2**20),
        cost_estimate=LIGHT,
        name="attend_forward",
    )(first, pre, pre, pre, scales, gains, cosine, sine, begin)


def attend_backward_kernel(first_ref, q_ref, k_ref, v_ref, o_ref, do_ref, lse_ref, qp_ref, kp_ref, scale_ref, gain_ref, cos_ref, sin_ref, begin_ref,
                           gq_ref, gk_ref, gv_ref, inner_ref, gain_grad_ref, kt_ref, dk_ref, dv_ref):
    blocks = q_ref.shape[0] // BLOCK
    norm = HEAD ** -0.5
    factor = norm * LOG2E

    def prepare(i, _):
        rows = pl.ds(pl.multiple_of(i * BLOCK, BLOCK), BLOCK)
        kt_ref[:, rows] = k_ref[rows, :].T
        dk_ref[rows, :] = jnp.zeros((BLOCK, HEAD), FULL)
        dv_ref[rows, :] = jnp.zeros((BLOCK, HEAD), FULL)
        return 0

    lax.fori_loop(0, blocks, prepare, 0)

    def finish(rows, n, grad, pre_ref, out):
        grad = grad.astype(LOW).astype(FULL)
        grad = grad * cos_ref[rows, :] - pltpu.roll(grad, HEAD // 2, 1) * sin_ref[rows, :]
        weighted = grad * gain_ref[n : n + 1, :]
        pre = pre_ref[rows, :]
        out[rows, :] = weighted
        inner_ref[0, n : n + 1, rows] = jnp.sum((weighted * pre).T, axis=0, keepdims=True)
        return jnp.sum(grad * pre * column(scale_ref[n : n + 1, rows]), axis=0, keepdims=True)

    def one(i, gain_grad):
        rows = pl.ds(pl.multiple_of(i * BLOCK, BLOCK), BLOCK)
        q = q_ref[rows, :]
        do = do_ref[rows, :]
        begin = begin_ref[0:1, rows]
        lse = lse_ref[0, 0:1, rows]
        delta = jnp.sum((do.astype(FULL) * o_ref[rows, :].astype(FULL)).T, axis=0, keepdims=True)
        at = lax.broadcasted_iota(jnp.int32, (BLOCK, BLOCK), 0)
        query_at = lax.broadcasted_iota(jnp.int32, (1, BLOCK), 1) + i * BLOCK

        def step(j, acc):
            keys = pl.ds(pl.multiple_of(j * BLOCK, BLOCK), BLOCK)
            s = dot_nt(k_ref[keys, :], q)
            key_at = at + j * BLOCK
            s = jnp.where((key_at >= begin) & (key_at <= query_at), s, NEG)
            p = jnp.exp2(s * factor - lse)
            dp = dot_nt(v_ref[keys, :], do)
            ds = (p * (dp - delta)).astype(LOW)
            dv_ref[keys, :] += dot(p.astype(LOW), do)
            dk_ref[keys, :] += dot(ds, q)
            return acc + dot(kt_ref[:, keys], ds)

        acc = lax.fori_loop(first_ref[i], i + 1, step, jnp.zeros((HEAD, BLOCK), FULL))
        return gain_grad + finish(rows, 0, acc.T * norm, qp_ref, gq_ref)

    gain_grad_ref[0:1, :] = lax.fori_loop(0, blocks, one, jnp.zeros((1, HEAD), FULL))

    def close(i, gain_grad):
        rows = pl.ds(pl.multiple_of(i * BLOCK, BLOCK), BLOCK)
        gv_ref[rows, :] = dv_ref[rows, :].astype(LOW)
        return gain_grad + finish(rows, 1, dk_ref[rows, :] * norm, kp_ref, gk_ref)

    gain_grad_ref[1:2, :] = lax.fori_loop(0, blocks, close, jnp.zeros((1, HEAD), FULL))


def attend_backward(head, q, k, v, out, grad, lse, pre, scales, gains, cosine, sine, first, begin):
    rows = q.shape[0]
    heads = pre.shape[1] // (3 * HEAD)

    def col(shift):
        return pl.BlockSpec((rows, HEAD), lambda i, f: (0, shift))

    def fixed(*shape):
        return pl.BlockSpec(shape, lambda i, f: (0,) * len(shape))

    full = jax.ShapeDtypeStruct((rows, HEAD), FULL)
    return pl.pallas_call(
        attend_backward_kernel,
        grid_spec=pltpu.PrefetchScalarGridSpec(
            num_scalar_prefetch=1,
            grid=(1,),
            in_specs=[col(head)] * 5
            + [
                pl.BlockSpec((1, 1, rows), lambda i, f: (head, 0, 0)),
                col(head),
                col(heads + head),
                fixed(2, rows),
                pl.BlockSpec((2, HEAD), lambda i, f: (0, head)),
                fixed(rows, HEAD),
                fixed(rows, HEAD),
                fixed(1, rows),
            ],
            out_specs=[fixed(rows, HEAD)] * 3 + [fixed(1, 2, rows), fixed(2, HEAD)],
            scratch_shapes=[
                pltpu.VMEM((HEAD, rows), LOW),
                pltpu.VMEM((rows, HEAD), FULL),
                pltpu.VMEM((rows, HEAD), FULL),
            ],
        ),
        out_shape=[
            full,
            full,
            jax.ShapeDtypeStruct((rows, HEAD), LOW),
            jax.ShapeDtypeStruct((1, 2, rows), FULL),
            jax.ShapeDtypeStruct((2, HEAD), FULL),
        ],
        compiler_params=pltpu.CompilerParams(vmem_limit_bytes=48 * 2**20),
        cost_estimate=LIGHT,
        name="attend_backward",
    )(first, q, k, v, out, grad, lse, pre, pre, scales, gains, cosine, sine, begin)


def per_device(
    tokens,
    cotangent,
    lengths,
    placement,
    w_query,
    w_key,
    w_value,
    w_output,
    query_gain,
    key_gain,
    attn_gain,
    w_gate,
    w_up,
    w_down,
    mlp_gain,
):
    data, seq = lax.axis_size("dp"), lax.axis_size("seq")
    seq_at = lax.axis_index("seq")
    _, count, width = tokens.shape
    row_len = count * seq
    own = width // seq
    row_ring = Ring([row_cycle(seq)])
    inputs = tokens.reshape(count, width)
    begin = layout(lengths, placement, row_len)

    packed = jnp.stack([w_query, w_key, w_value], axis=1).reshape(-1, 3, seq, own)
    packed = jnp.moveaxis(packed, 2, 0).reshape(seq, -1, 3 * own)
    hid = w_gate.shape[1]
    chips = data_bits(data)[:-1]
    state = {"gains": jnp.stack([query_gain, key_gain, attn_gain, mlp_gain])[None]}
    gain_bits = [b * seq for b in data_bits(data)] + bits_of(seq)
    gain_order = list(gain_bits)

    def more_gains():
        if gain_bits:
            state["gains"] = gain_step(state["gains"], gain_bits.pop(0))

    def beside(step, chunks):
        more_gains()
        if step == 1:
            state["down"] = swap_chips(w_down, chips)
            state["w_heads"] = lax.all_to_all(packed, "seq", split_axis=0, concat_axis=0, tiled=True)
            return ["gains"]
        if step == 2:
            return ["gains", "w_heads", "down", "begin"]
        if step == 3:
            state["w_heads"] = swap_chips(state["w_heads"].reshape(-1, 3 * own), chips)
            state["gate"], state["up"] = w_gate, w_up
            return ["gains", "w_heads", "gate", "up"]
        return ["gains"]

    state["begin"] = begin
    row_chunks = row_ring.gather(inputs, state, beside)
    begin = state["begin"]
    first_block = begin[::BLOCK] // BLOCK
    cosine, sine = rope_tables(jnp.arange(row_len, dtype=jnp.int32) - begin)
    begin = begin[None]
    state["gate"] = swap_chips(state["gate"], chips)
    last = row_ring.size // 2
    row_tokens = jnp.zeros((row_len, width), LOW)
    for offset, chunk in row_chunks.items():
        if offset == last:
            chunk, w_out, row_tokens, cosine, sine = tie(
                chunk, w_output, row_tokens, cosine, sine
            )
        row_tokens = lax.dynamic_update_slice(row_tokens, chunk, (row_ring.owner(offset) * count, 0))
    w_out = lax.all_gather(w_out, ("dp", "seq"), axis=0, tiled=True)
    w_heads = assemble((width, 3 * own), place_over_data(swap_cores(state["w_heads"])))
    pre = dot(row_tokens, w_heads)
    while gain_bits:
        more_gains()
    placed = [gain_order[::-1].index(bit) for bit in sorted(gain_order, reverse=True)]
    gains = state["gains"].reshape((2,) * len(placed) + state["gains"].shape[1:])
    gains = jnp.transpose(gains, [len(placed)] + placed + [len(placed) + 1])
    gains = gains.reshape(4, -1).astype(FULL)
    gain_attn, gain_mlp = gains[2], gains[3]
    gains_own = lax.dynamic_slice(gains, (0, seq_at * own), (2, own))
    query_pre, key_pre = pre[:, :own], pre[:, own : 2 * own]
    squares = jnp.stack([jnp.sum(query_pre * query_pre, axis=1), jnp.sum(key_pre * key_pre, axis=1)])
    scales = lax.rsqrt(sum_over(squares, "seq", seq) / width + EPSILON)
    scales, state["gate"], state["up"] = tie(scales, state["gate"], state["up"])
    state["up"] = swap_chips(state["up"], chips)
    attn_heads, query_rot, key_rot, values, log_sums = attend_forward(
        pre, scales, gains_own, cosine, sine, first_block, begin
    )
    attn_tokens = lax.all_to_all(
        attn_heads.reshape(seq, count, own), "seq", split_axis=0, concat_axis=0, tiled=True
    )
    attn_tokens = jnp.moveaxis(attn_tokens, 0, 1).reshape(count, width)

    attn_pre = dot(attn_tokens, w_out)
    attn_scale = rms_scale(attn_pre)
    middle = inputs.astype(FULL) + attn_pre * attn_scale * gain_attn
    middle_low = middle.astype(LOW)

    mids = row_ring.gather(middle_low)
    near, mids[0] = tie([state[n] for n in ("gate", "up", "down")], mids[0])
    near = [swap_cores(n) for n in near]
    gate_up = assemble((width, 2 * hid), place_over_data(near[0]) + place_over_data(near[1], 0, hid))
    down = assemble((hid, width), place_over_data(near[2], 1))
    saved = {}

    def mlp_part(offset):
        offset = offset if offset in mids else -offset
        both = dot(mids[offset], gate_up)
        gate, up = both[:, :hid], both[:, hid:]
        hidden = (gate * jax.nn.sigmoid(gate) * up).astype(LOW)
        saved[offset] = gate, up, hidden
        return dot(hidden, down)

    mlp_pre = row_ring.scatter(mlp_part)
    mlp_scale = rms_scale(mlp_pre)
    layer_out = (middle + mlp_pre * mlp_scale * gain_mlp).astype(LOW).reshape(tokens.shape)
    grad_final = cotangent.reshape(count, width).astype(FULL)
    grad_mlp_pre, grad_gain_mlp = norm_back(grad_final, mlp_pre, mlp_scale, gain_mlp)
    grads = row_ring.gather(grad_mlp_pre.astype(LOW))
    grad_both = {}

    def middle_part(offset):
        gate, up, hidden = saved[offset]
        grad_hidden = dot_nt(grads[offset], down)
        sig = jax.nn.sigmoid(gate)
        grad_gate = grad_hidden * up * sig * (1.0 + gate * (1.0 - sig))
        grad_up = grad_hidden * gate * sig
        grad_both[offset] = grad_gate.astype(LOW), grad_up.astype(LOW)
        return dot_nt(jnp.concatenate(grad_both[offset], axis=1), gate_up)

    order = list(mids)
    ffn = {"mids": jnp.concatenate([mids[o] for o in order])}
    ffn["grads"] = jnp.concatenate([grads[o] for o in order])
    ffn["hidden"] = jnp.concatenate([saved[o][2] for o in order])

    half = row_ring.size // 2

    def beside_middle(step, sent):
        if step == half - 2:
            ffn["down"] = dot_tn(ffn["hidden"], ffn["grads"]).astype(LOW)
            sent, ffn["down"] = tie(sent, ffn["down"])
        if step == half - 1:
            rows = jnp.concatenate([grad_both[o][0] for o in order])
            ffn["gate"] = dot_tn(ffn["mids"], rows).astype(LOW)
            sent, ffn["gate"], ffn["down"] = tie(sent, ffn["gate"], ffn["down"])
        return sent

    middle_parts = {o: middle_part(o) for o in order}
    grad_middle = row_ring.scatter(lambda o: middle_parts[o], beside_middle)
    rows = jnp.concatenate([grad_both[o][1] for o in order])
    ffn["up"] = dot_tn(ffn["mids"], rows).astype(LOW)
    sums = {n: scatter_over_data(blocks_over_data(ffn[n], a)) for n, a in (("down", 1), ("gate", 0))}
    grad_middle, sums, ffn["up"] = tie(grad_middle, sums, ffn["up"])
    grad_middle = grad_final + grad_middle

    grad_attn_pre, grad_gain_attn = norm_back(grad_middle, attn_pre, attn_scale, gain_attn)
    grad_attn_low = grad_attn_pre.astype(LOW)
    grad_heads = dot_nt(grad_attn_low, w_out).astype(LOW)
    grad_heads, grad_attn_low = tie(grad_heads, grad_attn_low)
    grad_heads = jnp.moveaxis(grad_heads.reshape(count, seq, own), 1, 0)
    grad_heads = lax.all_to_all(grad_heads, "seq", split_axis=0, concat_axis=0, tiled=True)
    grad_heads = grad_heads.reshape(row_len, own)
    steps = output_grad_steps(dot_tn(attn_tokens, grad_attn_low).astype(LOW), row_ring)
    sent = next(steps)
    sums["up"] = scatter_over_data(blocks_over_data(ffn["up"], 0))
    got = {n: last_over_data(sums[n][1]) for n in ("down", "gate")}
    grad_heads, sent, sums["up"] = tie(grad_heads, sent, sums["up"])
    got["up"] = last_over_data(sums["up"][1])
    sums = {n: val[0] for n, val in sums.items()}
    heads = []
    for head in range(own // HEAD):
        if head:
            sent = steps.send(sent)
            grad_heads, sent, *early = tie(grad_heads, sent, got["down"], got["gate"])
            got["down"], got["gate"] = early
        done = attend_backward(
            head,
            query_rot,
            key_rot,
            values,
            attn_heads,
            grad_heads,
            log_sums,
            pre,
            scales,
            gains_own,
            cosine,
            sine,
            first_block,
            begin,
        )
        heads.append(list(done))
    sent = steps.send(sent)
    weighted_q, weighted_k, grad_v = (
        jnp.concatenate([h[i] for h in heads], axis=1) for i in range(3)
    )
    inner = sum(h[3][0] for h in heads)
    inner, sent, got["up"] = tie(inner, sent, got["up"])
    gain_part = jnp.concatenate([h[4] for h in heads], axis=1)
    gain_part = lax.dynamic_update_slice(jnp.zeros((2, width), FULL), gain_part, (0, seq_at * own))
    inner = jnp.concatenate([inner, jnp.zeros((2, width - row_len), FULL)], axis=1)
    small = jnp.concatenate([inner, gain_part, grad_gain_attn[None], grad_gain_mlp[None]])
    small = sum_over(small, "seq", seq)
    inner, gain_sums = small[:2, :row_len], small[2:]
    last_sent = steps.send(sent)
    inner = inner * (scales**3) / width
    by_token = jnp.concatenate([scales, inner]).T
    grad_qp = by_token[:, 0:1] * weighted_q - by_token[:, 2:3] * query_pre
    grad_kp = by_token[:, 1:2] * weighted_k - by_token[:, 3:4] * key_pre
    grad_pre = jnp.concatenate([grad_qp.astype(LOW), grad_kp.astype(LOW), grad_v], axis=1)

    rest = {"pre": grad_pre, "output": last_sent, "sums": sums, "got": got}

    token_parts = dot_nt(grad_pre, w_heads).astype(LOW)

    def token_part(offset):
        start = row_ring.owner(offset) * count
        return lax.dynamic_slice_in_dim(token_parts, start, count, 0).astype(FULL)

    def beside_tokens(step, sent):
        names = ["pre"]
        if step == 1:
            names += ["sums", "got", "output"]
        if step == 2:
            rest["part"] = dot_tn(row_tokens, rest["pre"]).astype(LOW)
            names += ["part"]
        if step == 3:
            rest["part"] = scatter_over_data(blocks_over_data(rest["part"], 0))
            rest["part"] = rest["part"][0], last_over_data(rest["part"][1])
            names += ["part"]
        sent, *tied = tie(sent, *(rest[n] for n in names))
        rest.update(zip(names, tied))
        return sent

    grad_tokens = grad_middle + finish(
        row_ring.scatter_steps(token_part, lambda val: val), beside_tokens
    )
    grad_tokens = grad_tokens.astype(LOW).reshape(tokens.shape)
    gain_sums = sum_over(gain_sums, "dp", data)
    share = width // (data * seq)
    start = (lax.axis_index("dp") * seq + seq_at) * share
    gain_grads = lax.dynamic_slice(gain_sums, (0, start), (4, share))
    part = (rest["part"][0].astype(FULL) + rest["part"][1].astype(FULL)).astype(LOW)
    part = lax.all_to_all(
        part.reshape(seq, -1, 3 * own), "seq", split_axis=0, concat_axis=0, tiled=True
    )
    grad_query, grad_key, grad_value = (
        jnp.concatenate([part[d, :, n * own : (n + 1) * own] for d in range(seq)], axis=1).astype(FULL)
        for n in range(3)
    )
    sums, got = rest["sums"], rest["got"]
    grad_output = finish_output_grad(finish(steps, sent=rest["output"]))
    grad_down, grad_gate, grad_up = (
        sums[n].astype(FULL) + got[n].astype(FULL) for n in ("down", "gate", "up")
    )

    return (
        layer_out,
        grad_tokens,
        grad_query,
        grad_key,
        grad_value,
        grad_output,
        gain_grads[0],
        gain_grads[1],
        gain_grads[2],
        grad_gate,
        grad_up,
        grad_down,
        gain_grads[3],
    )


def solution(mesh):
    rows = P("dp", "seq", None)
    both = P(("dp", "seq"), None)
    flat = P(("dp", "seq"))
    return jax.shard_map(
        per_device,
        mesh=mesh,
        in_specs=(rows, rows, P(), P())
        + (both,) * 4
        + (flat,) * 3
        + (P("dp", "seq"), P("dp", "seq"), P("seq", "dp"), flat),
        out_specs=(rows, rows)
        + (both,) * 4
        + (flat,) * 3
        + (P("dp", "seq"), P("dp", "seq"), P("seq", "dp"), flat),
        check_vma=False,
    )
```

```python
import math

import jax
import jax.numpy as jnp
from jax import lax
from jax.experimental import pallas as pl
from jax.experimental.pallas import tpu as pltpu
from jax.sharding import PartitionSpec as P

HEAD = 128
LEVELS = 4
EPSILON = 1e-06
ROPE_BASE = 500000.0
LOW = jnp.bfloat16
FULL = jnp.float32
NEG = -1e30
LOG2E = math.log2(math.e)
LIGHT = pl.CostEstimate(flops=1, bytes_accessed=1, transcendentals=0)
BLOCK = 512


def dot(left, right):
    return jnp.dot(left, right, preferred_element_type=FULL)


def dot_nt(left, right):
    return lax.dot_general(left, right, (((1,), (1,)), ((), ())), preferred_element_type=FULL)


def dot_tn(left, right):
    return lax.dot_general(left, right, (((0,), (0,)), ((), ())), preferred_element_type=FULL)


def swap(val, axis, mask):
    size = lax.axis_size(axis)
    return lax.ppermute(val, axis, [(i, i ^ mask) for i in range(size)])


def swap_all(val, mask):
    size = lax.axis_size("dp") * lax.axis_size("seq")
    return lax.ppermute(val, ("dp", "seq"), [(i, i ^ mask) for i in range(size)])


def tie(*vals):
    return lax.optimization_barrier(vals)


def bits_of(size):
    return [1 << i for i in range(size.bit_length() - 1)]


def sum_over(val, axis, size):
    for bit in bits_of(size):
        val = val + swap(val, axis, bit)
    return val


class Ring:
    def __init__(self, cycles):
        self.size = len(cycles[0])
        self.forth = [(c[i], c[(i + 1) % self.size]) for c in cycles for i in range(self.size)]
        self.back = [(b, a) for a, b in self.forth]
        total = self.size * len(cycles)
        owners = [[0] * self.size for _ in range(total)]
        for c in cycles:
            for i, dev in enumerate(c):
                for off in range(self.size):
                    owners[dev][off] = c[(i + off) % self.size]
        self.owners = owners

    def owner(self, offset):
        at = lax.axis_index("seq")
        found = jnp.int32(self.owners[0][offset % self.size])
        for dev, row in enumerate(self.owners[1:], 1):
            found = lax.select(at == dev, jnp.int32(row[offset % self.size]), found)
        return found

    def right(self, val):
        return lax.ppermute(val, "seq", self.forth)

    def left(self, val):
        return lax.ppermute(val, "seq", self.back)

    def gather(self, own, state=None, between=None):
        half = self.size // 2
        chunks = {0: own}
        r = l = own
        for k in range(1, half):
            r, l = self.right(r), self.left(l)
            chunks[-k], chunks[k] = r, l
            names = between(k, chunks) if between else ()
            if names:
                r, l, *beside = tie(r, l, *(state[n] for n in names))
                state |= dict(zip(names, beside))
        mid = own.shape[0] // 2
        chunks[half] = jnp.concatenate([self.right(r[:mid]), self.left(l[mid:])], axis=0)
        return chunks

    def scatter_steps(self, part, hold=lax.optimization_barrier):
        half = self.size // 2
        far = part(half).astype(LOW)
        mid = far.shape[0] // 2
        r, l = yield far[:mid], far[mid:]
        r, l = self.right(r), self.left(l)
        zero = jnp.zeros((), LOW)
        r = lax.pad(r, zero, ((0, mid, 0), (0, 0, 0)))
        l = lax.pad(l, zero, ((mid, 0, 0), (0, 0, 0)))
        for k in range(half - 1, 0, -1):
            a = hold(part(k)) + r.astype(FULL)
            b = hold(part(-k)) + l.astype(FULL)
            r, l = yield a.astype(LOW), b.astype(LOW)
            r, l = self.right(r), self.left(l)
        return hold(part(0)) + r.astype(FULL) + l.astype(FULL)

    def scatter(self, part, hook=None):
        return finish(self.scatter_steps(part), hook)


def finish(steps, hook=None, sent=None, step=0):
    try:
        sent = next(steps) if sent is None else sent
        while True:
            sent = steps.send(hook(step, sent) if hook else sent)
            step += 1
    except StopIteration as end:
        return end.value


def row_cycle(size):
    if size % LEVELS or size == LEVELS:
        return list(range(size))
    cols = size // LEVELS
    walk = [(0, 0)]
    for z in range(LEVELS):
        span = list(range(1, cols))
        walk += [(z, x) for x in (span if z % 2 == 0 else span[::-1])]
    walk += [(z, 0) for z in range(LEVELS - 1, 0, -1)]
    return [z * cols + x for z, x in walk]


def data_bits(size):
    return [b for b in bits_of(size) if b != 1] + [1]


def swap_chips(shard, bits):
    copies = {0: shard}
    for bit in bits:
        copies |= {mask ^ bit: swap(val, "dp", bit) for mask, val in copies.items()}
    return copies


def swap_cores(copies):
    return copies | {mask ^ 1: swap(val, "dp", 1) for mask, val in copies.items()}


def assemble_kernel(plan, at_ref, *refs):
    out_ref, sems = refs[-2], refs[-1]
    copies = []
    for i, (source, row, rows) in enumerate(plan):
        cols = refs[source].shape[1]
        place = (
            pl.ds(pl.multiple_of(at_ref[2 * i], 16), rows),
            pl.ds(pl.multiple_of(at_ref[2 * i + 1], 128), cols),
        )
        copies.append(
            pltpu.make_async_copy(refs[source].at[pl.ds(row, rows), :], out_ref.at[place], sems.at[i])
        )
    for copy in copies:
        copy.start()
    for copy in copies:
        copy.wait()


def assemble(shape, pieces):
    arrays, plan, at = [], [], []
    for val, row, rows, to_row, to_col in pieces:
        known = [i for i, a in enumerate(arrays) if a is val]
        if not known:
            arrays.append(val)
        plan.append((known[0] if known else len(arrays) - 1, row, rows))
        at += [to_row, to_col]
    at = jnp.stack([jnp.asarray(a, jnp.int32) for a in at])
    return pl.pallas_call(
        lambda at_ref, *refs: assemble_kernel(plan, at_ref, *refs),
        grid_spec=pltpu.PrefetchScalarGridSpec(
            num_scalar_prefetch=1,
            grid=(1,),
            in_specs=[pl.BlockSpec(memory_space=pl.ANY)] * len(arrays),
            out_specs=pl.BlockSpec(shape, lambda i, at: (0, 0)),
            scratch_shapes=[pltpu.SemaphoreType.DMA((len(plan),))],
        ),
        out_shape=jax.ShapeDtypeStruct(shape, LOW),
        compiler_params=pltpu.CompilerParams(vmem_limit_bytes=40 * 2**20),
        cost_estimate=pl.CostEstimate(flops=0, bytes_accessed=4 * shape[0] * shape[1], transcendentals=0),
        name="assemble",
    )(at, *arrays)


def place_over_data(copies, axis=0, shift=0):
    me = lax.axis_index("dp")
    pieces = []
    for mask, val in copies.items():
        at = [shift, shift]
        at[axis] = (me ^ mask) * val.shape[axis]
        pieces.append((val, 0, val.shape[0], at[0], at[1]))
    return pieces


def blocks_over_data(val, axis):
    size = lax.axis_size("dp")
    part = val.shape[axis] // size
    return [
        lax.dynamic_slice_in_dim(val, (lax.axis_index("dp") ^ m) * part, part, axis) for m in range(size)
    ]


def scatter_over_data(blocks):
    order = data_bits(len(blocks))[::-1]
    blocks = dict(enumerate(blocks))
    for bit in order[:-1]:
        out = {}
        for m in [m for m in blocks if not m & bit]:
            out[m] = (blocks[m].astype(FULL) + swap(blocks[m ^ bit], "dp", bit).astype(FULL)).astype(LOW)
        blocks = out
    return blocks[0], blocks[order[-1]]


def last_over_data(sent):
    return swap(sent, "dp", data_bits(lax.axis_size("dp"))[0])


def gain_step(val, bit):
    me = lax.axis_index("dp") * lax.axis_size("seq") + lax.axis_index("seq")
    got = swap_all(val, bit)
    upper = (me // bit) % 2 == 1
    return jnp.concatenate([jnp.where(upper, got, val), jnp.where(upper, val, got)], axis=0)


def output_grad_steps(part, row_ring):
    data, seq = lax.axis_size("dp"), lax.axis_size("seq")
    me = lax.axis_index("dp")
    tall = data // 2
    width = part.shape[1]
    rows = part.shape[0] // (data * seq)
    part = part.reshape(tall, 2, seq, rows, width)
    kept = lax.dynamic_index_in_dim(part, me % 2, 1, False)
    sent = lax.dynamic_index_in_dim(part, 1 - me % 2, 1, False)
    kept = (kept.astype(FULL) + swap(sent, "dp", 1).astype(FULL)).astype(LOW)

    def block(offset):
        one = lax.dynamic_index_in_dim(kept, row_ring.owner(offset), 1, False)
        return one.reshape(tall * rows, width).astype(FULL)

    return row_ring.scatter_steps(block, lambda val: val)


def finish_output_grad(val):
    data = lax.axis_size("dp")
    me = lax.axis_index("dp")
    val = val.reshape(data // 2, -1, val.shape[1])
    _, rows, width = val.shape
    for bit in data_bits(data)[:-1][::-1]:
        upper = (me // bit) % 2
        val = val.reshape(2, val.shape[0] // 2, rows, width)
        kept = lax.dynamic_index_in_dim(val, upper, 0, False)
        sent = lax.dynamic_index_in_dim(val, 1 - upper, 0, False)
        val = kept + swap(sent, "dp", bit)
    return val.reshape(rows, width)


def rms_scale(vals):
    return lax.rsqrt(jnp.mean(vals * vals, axis=-1, keepdims=True) + EPSILON)


def norm_back(grad_out, pre, scale, gain):
    weighted = grad_out * gain
    inner = jnp.mean(weighted * pre, axis=-1, keepdims=True)
    grad_pre = scale * weighted - pre * (scale * scale * scale) * inner
    grad_gain = jnp.sum(grad_out * pre * scale, axis=0)
    return (grad_pre, grad_gain)


def rope_tables(positions):
    half = HEAD // 2
    freq = ROPE_BASE ** (-2.0 * jnp.arange(half, dtype=FULL) / HEAD)
    angle = positions.astype(FULL)[:, None] * freq[None, :]
    cosine, sine = jnp.cos(angle), jnp.sin(angle)
    return jnp.concatenate([cosine, cosine], 1), jnp.concatenate([-sine, sine], 1)


def layout(lengths, placement, row_len):
    stored, docs = lengths.shape
    rows = jnp.arange(placement.shape[0], dtype=jnp.int32)
    row = jnp.sum(jnp.where(rows == lax.axis_index("dp"), placement, 0))
    doc_lens = jnp.sum(
        jnp.where(jnp.arange(stored, dtype=jnp.int32)[:, None] == row, lengths, 0), axis=0
    )
    upto = jnp.arange(docs, dtype=jnp.int32)
    doc_ends = jnp.sum(jnp.where(upto[None, :] <= upto[:, None], doc_lens[None, :], 0), axis=1)
    at = jnp.arange(row_len, dtype=jnp.int32)
    passed = at[:, None] >= doc_ends[None, :]
    return jnp.max(jnp.where(passed, doc_ends[None, :], 0), axis=1)


def column(row):
    return jnp.broadcast_to(row, (HEAD, row.shape[1])).T

def attend_forward_kernel(
    first_ref,
    q_ref,
    k_ref,
    v_ref,
    scale_ref,
    gain_ref,
    cos_ref,
    sin_ref,
    begin_ref,
    out_ref,
    qr_ref,
    kr_ref,
    vl_ref,
    lse_ref,
    keys_ref,
    vt_ref,
):
    i = pl.program_id(0)
    rows = pl.ds(pl.multiple_of(i * BLOCK, BLOCK), BLOCK)
    heads = [slice(at, at + HEAD) for at in range(0, q_ref.shape[1], HEAD)]
    factor = HEAD**-0.5 * LOG2E
    for n, (src, dst) in enumerate(((q_ref, qr_ref), (k_ref, kr_ref))):
        scale = column(scale_ref[n : n + 1, :])
        for head in heads:
            x = src[:, head] * scale * gain_ref[n : n + 1, head]
            x = x * cos_ref[...] + pltpu.roll(x, HEAD // 2, 1) * sin_ref[...]
            dst[:, head] = x.astype(LOW)
    keys_ref[rows, :] = kr_ref[...]
    for head in heads:
        v = v_ref[:, head].astype(LOW)
        vl_ref[:, head] = v
        vt_ref[head, rows] = v.T
    begin = begin_ref[0:1, :]
    at = lax.broadcasted_iota(jnp.int32, (BLOCK, BLOCK), 0)
    query_at = lax.broadcasted_iota(jnp.int32, (1, BLOCK), 1) + i * BLOCK

    def step(j, carry):
        keys = pl.ds(pl.multiple_of(j * BLOCK, BLOCK), BLOCK)
        key_at = at + j * BLOCK
        keep = (key_at >= begin) & (key_at <= query_at)
        scores = [
            jnp.where(keep, dot_nt(keys_ref[keys, head], qr_ref[:, head]), NEG) for head in heads
        ]
        out = []
        for head, s, (top, total, acc) in zip(heads, scores, carry):
            new = jnp.maximum(top, jnp.max(s, axis=0, keepdims=True))
            p = jnp.exp2((s - new) * factor)
            shrink = jnp.exp2((top - new) * factor)
            total = total * shrink + jnp.sum(p, axis=0, keepdims=True)
            acc = acc * shrink + dot(vt_ref[head, keys], p.astype(LOW))
            out.append((new, total, acc))
        return tuple(out)

    start = (
        jnp.full((1, BLOCK), NEG, FULL),
        jnp.zeros((1, BLOCK), FULL),
        jnp.zeros((HEAD, BLOCK), FULL),
    )
    done = lax.fori_loop(first_ref[i], i + 1, step, (start,) * len(heads))
    for h, (top, total, acc) in enumerate(done):
        out_ref[:, heads[h]] = (acc / total).T.astype(LOW)
        lse_ref[h, 0:1, :] = top * factor + jnp.log2(total)


def attend_forward(pre, scales, gains, cosine, sine, first, begin):
    rows, wide = pre.shape
    own = wide // 3

    def part(cols, at=0):
        return pl.BlockSpec((BLOCK, cols), lambda i, f: (i, at))

    def along(*lead):
        return pl.BlockSpec((*lead, BLOCK), lambda i, f: (0,) * len(lead) + (i,))

    return pl.pallas_call(
        attend_forward_kernel,
        grid_spec=pltpu.PrefetchScalarGridSpec(
            num_scalar_prefetch=1,
            grid=(rows // BLOCK,),
            in_specs=[part(own), part(own, 1), part(own, 2), along(2)]
            + [pl.BlockSpec((2, own), lambda i, f: (0, 0)), part(HEAD), part(HEAD), along(1)],
            out_specs=[part(own)] * 4 + [along(own // HEAD, 1)],
            scratch_shapes=[pltpu.VMEM((rows, own), LOW), pltpu.VMEM((own, rows), LOW)],
        ),
        out_shape=[jax.ShapeDtypeStruct((rows, own), LOW)] * 4
        + [jax.ShapeDtypeStruct((own // HEAD, 1, rows), FULL)],
        compiler_params=pltpu.CompilerParams(vmem_limit_bytes=48 * 2**20),
        cost_estimate=LIGHT,
        name="attend_forward",
    )(first, pre, pre, pre, scales, gains, cosine, sine, begin)


def attend_backward_kernel(first_ref, q_ref, k_ref, v_ref, o_ref, do_ref, lse_ref, qp_ref, kp_ref, scale_ref, gain_ref, cos_ref, sin_ref, begin_ref,
                           gq_ref, gk_ref, gv_ref, inner_ref, gain_grad_ref, kt_ref, dk_ref, dv_ref):
    blocks = q_ref.shape[0] // BLOCK
    norm = HEAD ** -0.5
    factor = norm * LOG2E

    def prepare(i, _):
        rows = pl.ds(pl.multiple_of(i * BLOCK, BLOCK), BLOCK)
        kt_ref[:, rows] = k_ref[rows, :].T
        dk_ref[rows, :] = jnp.zeros((BLOCK, HEAD), FULL)
        dv_ref[rows, :] = jnp.zeros((BLOCK, HEAD), FULL)
        return 0

    lax.fori_loop(0, blocks, prepare, 0)

    def finish(rows, n, grad, pre_ref, out):
        grad = grad.astype(LOW).astype(FULL)
        grad = grad * cos_ref[rows, :] - pltpu.roll(grad, HEAD // 2, 1) * sin_ref[rows, :]
        weighted = grad * gain_ref[n : n + 1, :]
        pre = pre_ref[rows, :]
        out[rows, :] = weighted
        inner_ref[0, n : n + 1, rows] = jnp.sum((weighted * pre).T, axis=0, keepdims=True)
        return jnp.sum(grad * pre * column(scale_ref[n : n + 1, rows]), axis=0, keepdims=True)

    def one(i, gain_grad):
        rows = pl.ds(pl.multiple_of(i * BLOCK, BLOCK), BLOCK)
        q = q_ref[rows, :]
        do = do_ref[rows, :]
        begin = begin_ref[0:1, rows]
        lse = lse_ref[0, 0:1, rows]
        delta = jnp.sum((do.astype(FULL) * o_ref[rows, :].astype(FULL)).T, axis=0, keepdims=True)
        at = lax.broadcasted_iota(jnp.int32, (BLOCK, BLOCK), 0)
        query_at = lax.broadcasted_iota(jnp.int32, (1, BLOCK), 1) + i * BLOCK

        def step(j, acc):
            keys = pl.ds(pl.multiple_of(j * BLOCK, BLOCK), BLOCK)
            s = dot_nt(k_ref[keys, :], q)
            key_at = at + j * BLOCK
            s = jnp.where((key_at >= begin) & (key_at <= query_at), s, NEG)
            p = jnp.exp2(s * factor - lse)
            dp = dot_nt(v_ref[keys, :], do)
            ds = (p * (dp - delta)).astype(LOW)
            dv_ref[keys, :] += dot(p.astype(LOW), do)
            dk_ref[keys, :] += dot(ds, q)
            return acc + dot(kt_ref[:, keys], ds)

        acc = lax.fori_loop(first_ref[i], i + 1, step, jnp.zeros((HEAD, BLOCK), FULL))
        return gain_grad + finish(rows, 0, acc.T * norm, qp_ref, gq_ref)

    gain_grad_ref[0:1, :] = lax.fori_loop(0, blocks, one, jnp.zeros((1, HEAD), FULL))

    def close(i, gain_grad):
        rows = pl.ds(pl.multiple_of(i * BLOCK, BLOCK), BLOCK)
        gv_ref[rows, :] = dv_ref[rows, :].astype(LOW)
        return gain_grad + finish(rows, 1, dk_ref[rows, :] * norm, kp_ref, gk_ref)

    gain_grad_ref[1:2, :] = lax.fori_loop(0, blocks, close, jnp.zeros((1, HEAD), FULL))


def attend_backward(head, q, k, v, out, grad, lse, pre, scales, gains, cosine, sine, first, begin):
    rows = q.shape[0]
    heads = pre.shape[1] // (3 * HEAD)

    def col(shift):
        return pl.BlockSpec((rows, HEAD), lambda i, f: (0, shift))

    def fixed(*shape):
        return pl.BlockSpec(shape, lambda i, f: (0,) * len(shape))

    full = jax.ShapeDtypeStruct((rows, HEAD), FULL)
    return pl.pallas_call(
        attend_backward_kernel,
        grid_spec=pltpu.PrefetchScalarGridSpec(
            num_scalar_prefetch=1,
            grid=(1,),
            in_specs=[col(head)] * 5
            + [
                pl.BlockSpec((1, 1, rows), lambda i, f: (head, 0, 0)),
                col(head),
                col(heads + head),
                fixed(2, rows),
                pl.BlockSpec((2, HEAD), lambda i, f: (0, head)),
                fixed(rows, HEAD),
                fixed(rows, HEAD),
                fixed(1, rows),
            ],
            out_specs=[fixed(rows, HEAD)] * 3 + [fixed(1, 2, rows), fixed(2, HEAD)],
            scratch_shapes=[
                pltpu.VMEM((HEAD, rows), LOW),
                pltpu.VMEM((rows, HEAD), FULL),
                pltpu.VMEM((rows, HEAD), FULL),
            ],
        ),
        out_shape=[
            full,
            full,
            jax.ShapeDtypeStruct((rows, HEAD), LOW),
            jax.ShapeDtypeStruct((1, 2, rows), FULL),
            jax.ShapeDtypeStruct((2, HEAD), FULL),
        ],
        compiler_params=pltpu.CompilerParams(vmem_limit_bytes=48 * 2**20),
        cost_estimate=LIGHT,
        name="attend_backward",
    )(first, q, k, v, out, grad, lse, pre, pre, scales, gains, cosine, sine, begin)


def per_device(
    tokens,
    cotangent,
    lengths,
    placement,
    w_query,
    w_key,
    w_value,
    w_output,
    query_gain,
    key_gain,
    attn_gain,
    w_gate,
    w_up,
    w_down,
    mlp_gain,
):
    data, seq = lax.axis_size("dp"), lax.axis_size("seq")
    seq_at = lax.axis_index("seq")
    _, count, width = tokens.shape
    row_len = count * seq
    own = width // seq
    row_ring = Ring([row_cycle(seq)])
    inputs = tokens.reshape(count, width)
    begin = layout(lengths, placement, row_len)

    packed = jnp.stack([w_query, w_key, w_value], axis=1).reshape(-1, 3, seq, own)
    packed = jnp.moveaxis(packed, 2, 0).reshape(seq, -1, 3 * own)
    hid = w_gate.shape[1]
    chips = data_bits(data)[:-1]
    state = {"gains": jnp.stack([query_gain, key_gain, attn_gain, mlp_gain])[None]}
    gain_bits = [b * seq for b in data_bits(data)] + bits_of(seq)
    gain_order = list(gain_bits)

    def more_gains():
        if gain_bits:
            state["gains"] = gain_step(state["gains"], gain_bits.pop(0))

    def beside(step, chunks):
        more_gains()
        if step == 1:
            state["down"] = swap_chips(w_down, chips)
            state["w_heads"] = lax.all_to_all(packed, "seq", split_axis=0, concat_axis=0, tiled=True)
            return ["gains"]
        if step == 2:
            state["gate"] = swap_chips(w_gate, chips)
            return ["gains", "w_heads", "down", "gate", "begin"]
        if step == 3:
            state["w_heads"] = swap_chips(state["w_heads"].reshape(-1, 3 * own), chips)
            state["up"] = w_up
            return ["gains", "w_heads", "up"]
        return ["gains"]

    state["begin"] = begin
    row_chunks = row_ring.gather(inputs, state, beside)
    begin = state["begin"]
    first_block = begin[::BLOCK] // BLOCK
    cosine, sine = rope_tables(jnp.arange(row_len, dtype=jnp.int32) - begin)
    begin = begin[None]
    state["up"] = swap_chips(state["up"], chips)
    last = row_ring.size // 2
    row_tokens = jnp.zeros((row_len, width), LOW)
    for offset, chunk in row_chunks.items():
        if offset == last:
            chunk, w_out, row_tokens, cosine, sine = tie(
                chunk, w_output, row_tokens, cosine, sine
            )
        row_tokens = lax.dynamic_update_slice(row_tokens, chunk, (row_ring.owner(offset) * count, 0))
    w_out = lax.all_gather(w_out, ("dp", "seq"), axis=0, tiled=True)
    w_heads = assemble((width, 3 * own), place_over_data(swap_cores(state["w_heads"])))
    pre = dot(row_tokens, w_heads)
    while gain_bits:
        more_gains()
    placed = [gain_order[::-1].index(bit) for bit in sorted(gain_order, reverse=True)]
    gains = state["gains"].reshape((2,) * len(placed) + state["gains"].shape[1:])
    gains = jnp.transpose(gains, [len(placed)] + placed + [len(placed) + 1])
    gains = gains.reshape(4, -1).astype(FULL)
    gain_attn, gain_mlp = gains[2], gains[3]
    gains_own = lax.dynamic_slice(gains, (0, seq_at * own), (2, own))
    query_pre, key_pre = pre[:, :own], pre[:, own : 2 * own]
    squares = jnp.stack([jnp.sum(query_pre * query_pre, axis=1), jnp.sum(key_pre * key_pre, axis=1)])
    scales = lax.rsqrt(sum_over(squares, "seq", seq) / width + EPSILON)
    scales, state["up"] = tie(scales, state["up"])
    attn_heads, query_rot, key_rot, values, log_sums = attend_forward(
        pre, scales, gains_own, cosine, sine, first_block, begin
    )
    attn_tokens = lax.all_to_all(
        attn_heads.reshape(seq, count, own), "seq", split_axis=0, concat_axis=0, tiled=True
    )
    attn_tokens = jnp.moveaxis(attn_tokens, 0, 1).reshape(count, width)

    attn_pre = dot(attn_tokens, w_out)
    attn_scale = rms_scale(attn_pre)
    middle = inputs.astype(FULL) + attn_pre * attn_scale * gain_attn
    middle_low = middle.astype(LOW)

    mids = row_ring.gather(middle_low)
    near, mids[0] = tie([state[n] for n in ("gate", "up", "down")], mids[0])
    near = [swap_cores(n) for n in near]
    gate_up = assemble((width, 2 * hid), place_over_data(near[0]) + place_over_data(near[1], 0, hid))
    down = assemble((hid, width), place_over_data(near[2], 1))
    saved = {}

    def mlp_part(offset):
        offset = offset if offset in mids else -offset
        both = dot(mids[offset], gate_up)
        gate, up = both[:, :hid], both[:, hid:]
        hidden = (gate * jax.nn.sigmoid(gate) * up).astype(LOW)
        saved[offset] = gate, up, hidden
        return dot(hidden, down)

    mlp_pre = row_ring.scatter(mlp_part)
    mlp_scale = rms_scale(mlp_pre)
    layer_out = (middle + mlp_pre * mlp_scale * gain_mlp).astype(LOW).reshape(tokens.shape)
    grad_final = cotangent.reshape(count, width).astype(FULL)
    grad_mlp_pre, grad_gain_mlp = norm_back(grad_final, mlp_pre, mlp_scale, gain_mlp)
    grads = row_ring.gather(grad_mlp_pre.astype(LOW))
    grad_both = {}

    def middle_part(offset):
        gate, up, hidden = saved[offset]
        grad_hidden = dot_nt(grads[offset], down)
        sig = jax.nn.sigmoid(gate)
        grad_gate = grad_hidden * up * sig * (1.0 + gate * (1.0 - sig))
        grad_up = grad_hidden * gate * sig
        grad_both[offset] = grad_gate.astype(LOW), grad_up.astype(LOW)
        return dot_nt(jnp.concatenate(grad_both[offset], axis=1), gate_up)

    order = list(mids)
    ffn = {"mids": jnp.concatenate([mids[o] for o in order])}
    ffn["grads"] = jnp.concatenate([grads[o] for o in order])
    ffn["hidden"] = jnp.concatenate([saved[o][2] for o in order])

    half = row_ring.size // 2

    def beside_middle(step, sent):
        if step == half - 2:
            ffn["down"] = dot_tn(ffn["hidden"], ffn["grads"]).astype(LOW)
            sent, ffn["down"] = tie(sent, ffn["down"])
        if step == half - 1:
            rows = jnp.concatenate([grad_both[o][0] for o in order])
            ffn["gate"] = dot_tn(ffn["mids"], rows).astype(LOW)
            sent, ffn["gate"], ffn["down"] = tie(sent, ffn["gate"], ffn["down"])
        return sent

    middle_parts = {o: middle_part(o) for o in order}
    grad_middle = row_ring.scatter(lambda o: middle_parts[o], beside_middle)
    rows = jnp.concatenate([grad_both[o][1] for o in order])
    ffn["up"] = dot_tn(ffn["mids"], rows).astype(LOW)
    sums = {n: scatter_over_data(blocks_over_data(ffn[n], a)) for n, a in (("down", 1), ("gate", 0))}
    grad_middle, sums, ffn["up"] = tie(grad_middle, sums, ffn["up"])
    grad_middle = grad_final + grad_middle

    grad_attn_pre, grad_gain_attn = norm_back(grad_middle, attn_pre, attn_scale, gain_attn)
    grad_attn_low = grad_attn_pre.astype(LOW)
    grad_heads = dot_nt(grad_attn_low, w_out).astype(LOW)
    grad_heads, grad_attn_low = tie(grad_heads, grad_attn_low)
    grad_heads = jnp.moveaxis(grad_heads.reshape(count, seq, own), 1, 0)
    grad_heads = lax.all_to_all(grad_heads, "seq", split_axis=0, concat_axis=0, tiled=True)
    grad_heads = grad_heads.reshape(row_len, own)
    steps = output_grad_steps(dot_tn(attn_tokens, grad_attn_low).astype(LOW), row_ring)
    sent = next(steps)
    sums["up"] = scatter_over_data(blocks_over_data(ffn["up"], 0))
    got = {n: last_over_data(sums[n][1]) for n in ("down", "gate")}
    grad_heads, sent, sums["up"] = tie(grad_heads, sent, sums["up"])
    got["up"] = last_over_data(sums["up"][1])
    sums = {n: val[0] for n, val in sums.items()}
    heads = []
    for head in range(own // HEAD):
        if head:
            sent = steps.send(sent)
            grad_heads, sent, *early = tie(grad_heads, sent, got["down"], got["gate"])
            got["down"], got["gate"] = early
        done = attend_backward(
            head,
            query_rot,
            key_rot,
            values,
            attn_heads,
            grad_heads,
            log_sums,
            pre,
            scales,
            gains_own,
            cosine,
            sine,
            first_block,
            begin,
        )
        heads.append(list(done))
    sent = steps.send(sent)
    weighted_q, weighted_k, grad_v = (
        jnp.concatenate([h[i] for h in heads], axis=1) for i in range(3)
    )
    inner = sum(h[3][0] for h in heads)
    inner, sent, got["up"] = tie(inner, sent, got["up"])
    gain_part = jnp.concatenate([h[4] for h in heads], axis=1)
    gain_part = lax.dynamic_update_slice(jnp.zeros((2, width), FULL), gain_part, (0, seq_at * own))
    inner = jnp.concatenate([inner, jnp.zeros((2, width - row_len), FULL)], axis=1)
    small = jnp.concatenate([inner, gain_part, grad_gain_attn[None], grad_gain_mlp[None]])
    small = sum_over(small, "seq", seq)
    inner, gain_sums = small[:2, :row_len], small[2:]
    last_sent = steps.send(sent)
    inner = inner * (scales**3) / width
    by_token = jnp.concatenate([scales, inner]).T
    grad_qp = by_token[:, 0:1] * weighted_q - by_token[:, 2:3] * query_pre
    grad_kp = by_token[:, 1:2] * weighted_k - by_token[:, 3:4] * key_pre
    grad_pre = jnp.concatenate([grad_qp.astype(LOW), grad_kp.astype(LOW), grad_v], axis=1)

    rest = {"pre": grad_pre, "output": last_sent, "sums": sums, "got": got}

    token_parts = dot_nt(grad_pre, w_heads).astype(LOW)

    def token_part(offset):
        start = row_ring.owner(offset) * count
        return lax.dynamic_slice_in_dim(token_parts, start, count, 0).astype(FULL)

    def beside_tokens(step, sent):
        names = ["pre"]
        if step == 1:
            names += ["sums", "got", "output"]
        if step == 2:
            rest["part"] = dot_tn(row_tokens, rest["pre"]).astype(LOW)
            names += ["part"]
        if step == 3:
            rest["part"] = scatter_over_data(blocks_over_data(rest["part"], 0))
            rest["part"] = rest["part"][0], last_over_data(rest["part"][1])
            names += ["part"]
        sent, *tied = tie(sent, *(rest[n] for n in names))
        rest.update(zip(names, tied))
        return sent

    grad_tokens = grad_middle + finish(
        row_ring.scatter_steps(token_part, lambda val: val), beside_tokens
    )
    grad_tokens = grad_tokens.astype(LOW).reshape(tokens.shape)
    gain_sums = sum_over(gain_sums, "dp", data)
    share = width // (data * seq)
    start = (lax.axis_index("dp") * seq + seq_at) * share
    gain_grads = lax.dynamic_slice(gain_sums, (0, start), (4, share))
    part = (rest["part"][0].astype(FULL) + rest["part"][1].astype(FULL)).astype(LOW)
    part = lax.all_to_all(
        part.reshape(seq, -1, 3 * own), "seq", split_axis=0, concat_axis=0, tiled=True
    )
    grad_query, grad_key, grad_value = (
        jnp.concatenate([part[d, :, n * own : (n + 1) * own] for d in range(seq)], axis=1).astype(FULL)
        for n in range(3)
    )
    sums, got = rest["sums"], rest["got"]
    grad_output = finish_output_grad(finish(steps, sent=rest["output"]))
    grad_down, grad_gate, grad_up = (
        sums[n].astype(FULL) + got[n].astype(FULL) for n in ("down", "gate", "up")
    )

    return (
        layer_out,
        grad_tokens,
        grad_query,
        grad_key,
        grad_value,
        grad_output,
        gain_grads[0],
        gain_grads[1],
        gain_grads[2],
        grad_gate,
        grad_up,
        grad_down,
        gain_grads[3],
    )


def solution(mesh):
    rows = P("dp", "seq", None)
    both = P(("dp", "seq"), None)
    flat = P(("dp", "seq"))
    return jax.shard_map(
        per_device,
        mesh=mesh,
        in_specs=(rows, rows, P(), P())
        + (both,) * 4
        + (flat,) * 3
        + (P("dp", "seq"), P("dp", "seq"), P("seq", "dp"), flat),
        out_specs=(rows, rows)
        + (both,) * 4
        + (flat,) * 3
        + (P("dp", "seq"), P("dp", "seq"), P("seq", "dp"), flat),
        check_vma=False,
    )
```
